256 devices in a mesh: node: 32 (over z, x), feat: 8 (over y, core).
Axes of the slice: x: 4, y: 4, z: 8, core: 2. Of those that a mesh axis runs over, the one named last changes fastest.
Arguments:
- features: bfloat16 [262144, 256], P(('node', 'feat')), may hold values from -6 to 6
- weight: bfloat16 [256, 256], replicated, may hold values from -0.375 to 0.375
- adjacency: bfloat16 [16384, 128, 128], P('node'), may hold values from 0 to 0.076171875
- block_coords: int32 [2, 16384], P(None, 'node'), may hold values from 0 to 127, as said below
- block_counts: int32 [32], P('node'), may hold values from 128 to 512, as said below
- send_rows: int32 [1024, 256], P('node'), may hold values from 0 to 8191, as said below
- cotangent: bfloat16 [256, 262144], P('feat', 'node'), may hold values from -6 to 6
Outputs:
- activations: bfloat16 [256, 262144], P('feat', 'node')
- input_grad: bfloat16 [262144, 256], P(('node', 'feat'))
- weight_grad: float32 [256, 256], P(None, 'feat')
The draws below stay inside these ranges and needn't reach their ends.
Inputs may be any that keep to these rules, and one draw needn't show every extreme that they name: `send_rows`: row q * 32 + p lists 256 distinct local rows (0 to 8191) of partition q sent to partition p. `block_coords`: per partition, slots 0 to 63 hold the diagonal blocks (r, r); slots 64 to 127 hold one block with column block 64 + h for each h; row blocks lie in 0 to 63, column blocks in 0 to 127; coordinates may repeat. `block_counts`: between 128 and 512; some partition has exactly 512.
All inputs are finite; a program needn't handle non-finite values.
Results may differ from the reference program's by a relative error of at most 0.0061.
Values may be sent and summed in bfloat16 or wider, within the bound.
A program may use at most 128 MiB of HBM per device.

```python
import math
import jax
import jax.numpy as jnp
from jax import lax

F = 256
BLK = 128
ROWB = 64
HP = 256
HALOB = 64
MAXB = 512
BLOCKS_ALL = 16384
LISTS = 1024
NODES = 262144
N_NODE = 32


def draw_block_coords(key, part):
    key = jax.random.fold_in(key, 11)
    nparts = BLOCKS_ALL // MAXB
    first_key, second_key = jax.random.split(key)
    slots = jnp.arange(MAXB, dtype=jnp.int32)[None, :]
    rand_rows = jax.random.randint(first_key, (nparts, MAXB), 0, ROWB, dtype=jnp.int32)
    rand_cols = jax.random.randint(second_key, (nparts, MAXB), 0, ROWB + HALOB, dtype=jnp.int32)
    block_rows = jnp.where(slots < ROWB, slots, rand_rows)
    block_cols = jnp.where(slots < ROWB + HALOB, slots, rand_cols)
    return jnp.stack([block_rows.reshape(-1), block_cols.reshape(-1)]).astype(jnp.int32)


def draw_block_counts(key, part):
    key = jax.random.fold_in(key, 12)
    nparts = BLOCKS_ALL // MAXB
    first_key, second_key = jax.random.split(key)
    uniform_ints = jax.random.randint(first_key, (nparts,), 0, 1001, dtype=jnp.int32)
    counts = MAXB // 4 + 3 * MAXB // 4 * (uniform_ints * uniform_ints // 1000) // 1000
    chosen = jax.random.randint(second_key, (), 0, nparts, dtype=jnp.int32)
    counts = jnp.where(jnp.arange(nparts, dtype=jnp.int32) == chosen, MAXB, counts)
    return counts.astype(jnp.int32)


def draw_send_rows(key, part):
    key = jax.random.fold_in(key, 13)
    keys = jax.random.split(key, LISTS)

    def one_list(list_key):
        order = jax.random.permutation(list_key, BLK * ROWB)
        return jnp.sort(order[:HP])
    return jax.vmap(one_list)(keys).astype(jnp.int32)


def block_levels(stream_key, extent, shards, low, high):
    def one(axis_at, blocks):
        steps = jax.random.uniform(jax.random.fold_in(jax.random.fold_in(stream_key, 6), axis_at), (blocks,), jnp.float32, low / len(shards), high / len(shards))
        return jnp.repeat(jnp.exp(steps), extent[axis_at] // blocks).reshape((-1,) + (1,) * (len(extent) - axis_at - 1))

    loudness = one(*shards[0])
    for cut in shards[1:]:
        loudness = loudness * one(*cut)
    return loudness


def noise(own_key, extent, scale, most, cuts=(), kind=jnp.bfloat16):
    loudness = block_levels(own_key, extent, cuts, -0.22, 0.18) if cuts else 1.0
    drawn = jax.random.normal(own_key, extent, jnp.float32) * scale * loudness
    return jnp.minimum(jnp.maximum(drawn, -most), most).astype(kind)


def setup_inputs(seed: int = 0) -> dict:
    streams_of = jax.random.split(jax.random.key(seed), 8)
    return {
        "features": noise(streams_of[0], (NODES, F), 1.0, 6.0, ((0, 256),)),
        "weight": noise(streams_of[1], (F, F), F ** -0.5, 0.375),
        "adjacency": jnp.clip(0.076171875 * jax.random.uniform(streams_of[2], (BLOCKS_ALL, BLK, BLK), jnp.float32) ** block_levels(streams_of[2], (BLOCKS_ALL, BLK, BLK), ((0, 32),), -0.2, 0.2), 0.0, 0.076171875).astype(jnp.bfloat16),
        "block_coords": draw_block_coords(jax.random.fold_in(streams_of[7], 71), 0),
        "block_counts": draw_block_counts(jax.random.fold_in(streams_of[7], 71), 0),
        "send_rows": draw_send_rows(jax.random.fold_in(streams_of[7], 71), 0),
        "cotangent": noise(streams_of[6], (F, NODES), 1.0, 6.0, ((0, 8), (1, 32))),
    }


def aggregate(extended, block_rows, block_cols, blocks, count):
    max_blocks = blocks.shape[0]
    block_size = blocks.shape[1]
    width = extended.shape[0]
    active = jnp.arange(max_blocks, dtype=jnp.int32) < count
    tiles = extended.reshape(width, -1, block_size)
    picked = jnp.take(tiles, block_cols, axis=1).astype(jnp.float32)
    products = jnp.einsum('fbj,bij->fbi', picked, blocks.astype(jnp.float32))
    row_hot = ((block_rows[:, None] == jnp.arange(ROWB, dtype=jnp.int32)[None, :]) & active[:, None]).astype(jnp.float32)
    summed = jnp.einsum('fbi,br->fri', products, row_hot, precision=lax.Precision.HIGHEST)
    return summed.reshape(width, ROWB * block_size)

def spread_back(grad_pre, block_rows, block_cols, blocks, count):
    max_blocks = blocks.shape[0]
    block_size = blocks.shape[1]
    width = grad_pre.shape[0]
    active = (jnp.arange(max_blocks, dtype=jnp.int32) < count).astype(grad_pre.dtype)
    tiles = grad_pre.reshape(width, -1, block_size)
    picked = jnp.take(tiles, block_rows, axis=1) * active[None, :, None]
    contrib = jnp.einsum('fbi,bij->fbj', picked.astype(jnp.float32), blocks.astype(jnp.float32))
    col_hot = (block_cols[:, None] == jnp.arange(ROWB + HALOB, dtype=jnp.int32)[None, :]).astype(jnp.float32)
    spread = jnp.einsum('fbj,bc->fcj', contrib, col_hot, precision=lax.Precision.HIGHEST)
    return spread.reshape(width, (ROWB + HALOB) * block_size)

def reference(features, weight, adjacency, block_coords, block_counts, send_rows, cotangent):
    nparts = N_NODE
    part_rows = BLK * ROWB
    projected = jnp.dot(features, weight, preferred_element_type=jnp.float32).astype(jnp.bfloat16)
    lists = send_rows.reshape(nparts, nparts, HP)
    global_rows = (jnp.arange(nparts, dtype=jnp.int32)[:, None, None] * part_rows + lists).astype(jnp.int32)
    block_sets = adjacency.reshape(nparts, MAXB, BLK, BLK)
    coord_rows = block_coords[0].reshape(nparts, MAXB)
    coord_cols = block_coords[1].reshape(nparts, MAXB)
    cot_parts = cotangent.reshape(F, nparts, part_rows).transpose(1, 0, 2)

    def one_part(inputs):
        index, blocks, rows_here, cols_here, count, cot_here = inputs
        start = (index * part_rows).astype(jnp.int32)
        owned = lax.dynamic_slice_in_dim(projected, start, part_rows, 0).T
        halo = jnp.take(projected, global_rows[:, index, :].reshape(-1), axis=0).T
        extended = jnp.concatenate([owned, halo], axis=1)
        preact = aggregate(extended, rows_here, cols_here, blocks, count)
        sigma = jax.nn.sigmoid(preact)
        act = (preact * sigma).astype(jnp.bfloat16)
        grad_pre = (cot_here.astype(jnp.float32) * sigma * (1.0 + preact * (1.0 - sigma))).astype(jnp.bfloat16)
        grad_ext = spread_back(grad_pre, rows_here, cols_here, blocks, count)
        return (act, grad_ext[:, :part_rows], grad_ext[:, part_rows:])
    acts, local_grads, halo_grads = lax.map(one_part, (jnp.arange(nparts, dtype=jnp.int32), block_sets, coord_rows, coord_cols, block_counts, cot_parts))
    activations = acts.transpose(1, 0, 2).reshape(F, nparts * part_rows)
    grad_sum = local_grads.transpose(0, 2, 1).reshape(nparts * part_rows, F)
    values = halo_grads.reshape(nparts, F, nparts, HP).transpose(0, 2, 3, 1).reshape(-1, F)
    targets = global_rows.transpose(1, 0, 2).reshape(-1)
    grad_sum = grad_sum.at[targets].add(values)
    grad_z = grad_sum.astype(jnp.bfloat16)
    input_grad = jnp.dot(grad_z, weight.T, preferred_element_type=jnp.float32).astype(jnp.bfloat16)
    weight_grad = jnp.dot(features.T, grad_z, preferred_element_type=jnp.float32) * (1.0 / math.sqrt(nparts * part_rows))
    return (activations, input_grad, weight_grad)
```

```python
import functools
import math

import jax
import jax.numpy as jnp
from jax import lax
from jax.experimental import pallas as pl
from jax.experimental.pallas import tpu as pltpu
from jax.sharding import PartitionSpec as P

ZS, XS = 8, 4
NN = ZS * XS
NF = 8
F = 256
CW = F // NF
RD = 1024
LO = 256
GD = RD // LO
GP = NF * GD
HP = 256
BLK = 128
ROWB = 64
COLB = 128
MAXB = 512
MESH = pl.DeviceIdType.MESH
VMEM = pltpu.VMEM


def node_at(n, k):
    z = lax.rem(lax.div(n, XS) + lax.div(k, XS), ZS)
    x = lax.rem(lax.rem(n, XS) + lax.rem(k, XS), XS)
    return z * XS + x


def node_back(n, k):
    z = lax.rem(lax.div(n, XS) + ZS - lax.div(k, XS), ZS)
    x = lax.rem(lax.rem(n, XS) + XS - lax.rem(k, XS), XS)
    return z * XS + x


def enter(n, f):
    barrier = pltpu.get_barrier_semaphore()

    def greet_node(k, c):
        pl.semaphore_signal(barrier, inc=1, device_id={"node": node_at(n, k)}, device_id_type=MESH)
        return c

    def greet_feat(k, c):
        pl.semaphore_signal(barrier, inc=1, device_id={"feat": lax.rem(f + k, NF)}, device_id_type=MESH)
        return c

    lax.fori_loop(1, NF, greet_feat, 0)
    lax.fori_loop(1, NN, greet_node, 0)
    return barrier


def one_hot_t(lists, p):
    idx = lists[pl.ds(p, 1), :]
    lo = idx & (LO - 1)
    hi = lax.shift_right_logical(idx, 8)
    rows = lax.broadcasted_iota(jnp.int32, (LO, HP), 0)
    return (rows == lo).astype(jnp.float32).astype(jnp.bfloat16), hi


def forward_kernel(
    x_ref, w_ref, lists, own, halo, proj, packed, fsend, frecv, nsend, nrecv
):
    n = lax.axis_index("node")
    f = lax.axis_index("feat")
    barrier = enter(n, f)
    wt = w_ref[...].astype(jnp.float32).T.astype(jnp.bfloat16)
    for h in range(GD):
        proj[h] = lax.dot_general(
            wt,
            x_ref[h * LO : (h + 1) * LO, :],
            (((1,), (1,)), ((), ())),
            preferred_element_type=jnp.float32,
        ).astype(jnp.bfloat16)
    pl.semaphore_wait(barrier, NN + NF - 2)

    def feat_copy(k, to, source):
        return pltpu.make_async_remote_copy(
            src_ref=proj.at[:, pl.ds(pl.multiple_of(to * CW, CW), CW), :],
            dst_ref=own.at[pl.ds(source * GD, GD)],
            send_sem=fsend.at[k],
            recv_sem=frecv.at[k],
            device_id={"feat": to},
            device_id_type=MESH,
        )

    def start_feat(k, c):
        feat_copy(k, lax.rem(f + k, NF), f).start()
        return c

    lax.fori_loop(1, NF, start_feat, 0)
    own[pl.ds(f * GD, GD)] = proj[:, pl.ds(pl.multiple_of(f * CW, CW), CW), :]

    def wait_feat(k, c):
        feat_copy(k, lax.rem(f + k, NF), lax.rem(f + NF - k, NF)).wait_recv()
        return c

    lax.fori_loop(1, NF, wait_feat, 0)

    def pick(p):
        hot, hi = one_hot_t(lists, p)
        got = jnp.zeros((CW, HP), jnp.float32)
        step = 8
        for g in range(0, GP, step):
            part = jnp.dot(
                own[g : g + step].reshape(step * CW, LO), hot, preferred_element_type=jnp.float32
            )
            for h in range(step):
                got = jnp.where(hi == g + h, part[h * CW : (h + 1) * CW], got)
        return got.astype(jnp.bfloat16)

    def node_copy(k, to, source):
        return pltpu.make_async_remote_copy(
            src_ref=packed.at[k],
            dst_ref=halo.at[source],
            send_sem=nsend.at[k],
            recv_sem=nrecv.at[k],
            device_id={"node": to},
            device_id_type=MESH,
        )

    def send_node(i, c):
        k = NN - i
        to = node_at(n, k)
        packed[k] = pick(to)
        node_copy(k, to, n).start()
        return c

    lax.fori_loop(1, NN, send_node, 0)
    halo[n] = pick(n)

    def finish_node(i, c):
        k = NN - i
        node_copy(k, node_at(n, k), node_back(n, k)).wait()
        return c

    lax.fori_loop(1, NN, finish_node, 0)

    def finish_feat(k, c):
        feat_copy(k, lax.rem(f + k, NF), f).wait_send()
        return c

    lax.fori_loop(1, NF, finish_feat, 0)


def forward(features, weight, lists):
    part = jax.ShapeDtypeStruct((GP, CW, LO), jnp.bfloat16)
    return pl.pallas_call(
        forward_kernel,
        out_shape=(part, part),
        in_specs=[pl.BlockSpec(memory_space=VMEM)] * 3,
        out_specs=(pl.BlockSpec(memory_space=VMEM),) * 2,
        scratch_shapes=[
            VMEM((GD, F, LO), jnp.bfloat16),
            VMEM((NN, CW, HP), jnp.bfloat16),
            pltpu.SemaphoreType.DMA((NF,)),
            pltpu.SemaphoreType.DMA((NF,)),
            pltpu.SemaphoreType.DMA((NN,)),
            pltpu.SemaphoreType.DMA((NN,)),
        ],
        compiler_params=pltpu.CompilerParams(
            collective_id=0, has_side_effects=True, vmem_limit_bytes=32 * 2**20
        ),
        name="project_and_send",
    )(features, weight, lists)


CHUNKS = 16
PER_CHUNK = MAXB // CHUNKS
UNROLL = 8


def blocks_kernel(
    coords, counts, adj, own, halo, cot, act, local, remote, held, ext, pre, gpre, grad, sems
):
    def chunk(i):
        rows = pl.ds(i * PER_CHUNK, PER_CHUNK)
        return pltpu.make_async_copy(adj.at[rows], held.at[rows], sems.at[i])

    for i in range(CHUNKS):
        chunk(i).start()
    count = counts[0]
    pre[...] = jnp.zeros_like(pre)
    for g in range(GP):
        for s in range(2):
            ext[2 * g + s] = own[g, :, s * BLK : (s + 1) * BLK]
            ext[ROWB + 2 * g + s] = halo[g, :, s * BLK : (s + 1) * BLK]

    def row_of(b):
        return jnp.where(b < count, coords[0, b], ROWB)

    def gather_chunk(i, c):
        chunk(i).wait()

        def some(j, c):
            base = i * PER_CHUNK + j * UNROLL
            terms = []
            for u in range(UNROLL):
                b = base + u
                terms.append(
                    lax.dot_general(
                        ext[coords[1, b]],
                        held[b],
                        (((1,), (1,)), ((), ())),
                        preferred_element_type=jnp.float32,
                    )
                )
            for u in range(UNROLL):
                r = row_of(base + u)
                pre[r] = pre[r] + terms[u]
            return c

        return lax.fori_loop(0, PER_CHUNK // UNROLL, some, c)

    lax.fori_loop(0, CHUNKS, gather_chunk, 0)

    for r in range(ROWB):
        v = pre[r]
        at = slice(r * BLK, (r + 1) * BLK)
        sigma = jax.nn.sigmoid(v)
        act[:, at] = (v * sigma).astype(jnp.bfloat16)
        gpre[r] = (cot[:, at].astype(jnp.float32) * sigma * (1.0 + v * (1.0 - sigma))).astype(
            jnp.bfloat16
        )
    gpre[ROWB] = jnp.zeros((CW, BLK), jnp.bfloat16)
    grad[...] = jnp.zeros_like(grad)

    def spread(j, c):
        base = j * UNROLL
        terms = []
        for u in range(UNROLL):
            b = base + u
            terms.append(jnp.dot(gpre[row_of(b)], held[b], preferred_element_type=jnp.float32))
        for u in range(UNROLL):
            col = coords[1, base + u]
            grad[col] = grad[col] + terms[u]
        return c

    lax.fori_loop(0, MAXB // UNROLL, spread, 0)
    for g in range(GP):
        for s in range(2):
            at = slice(s * BLK, (s + 1) * BLK)
            local[g, :, at] = grad[2 * g + s]
            remote[g, :, at] = grad[ROWB + 2 * g + s].astype(jnp.bfloat16)


def blocks(coords, counts, adjacency, own, halo, cotangent):
    return pl.pallas_call(
        blocks_kernel,
        out_shape=(
            jax.ShapeDtypeStruct((CW, ROWB * BLK), jnp.bfloat16),
            jax.ShapeDtypeStruct((GP, CW, LO), jnp.float32),
            jax.ShapeDtypeStruct((NN, CW, HP), jnp.bfloat16),
        ),
        in_specs=[
            pl.BlockSpec(memory_space=pltpu.SMEM),
            pl.BlockSpec(memory_space=pltpu.SMEM),
            pl.BlockSpec(memory_space=pl.ANY),
            pl.BlockSpec(memory_space=VMEM),
            pl.BlockSpec(memory_space=VMEM),
            pl.BlockSpec(memory_space=VMEM),
        ],
        out_specs=(pl.BlockSpec(memory_space=VMEM),) * 3,
        scratch_shapes=[
            VMEM((MAXB, BLK, BLK), jnp.bfloat16),
            VMEM((COLB, CW, BLK), jnp.bfloat16),
            VMEM((ROWB + 1, CW, BLK), jnp.float32),
            VMEM((ROWB + 1, CW, BLK), jnp.bfloat16),
            VMEM((COLB, CW, BLK), jnp.float32),
            pltpu.SemaphoreType.DMA((CHUNKS,)),
        ],
        compiler_params=pltpu.CompilerParams(vmem_limit_bytes=40 * 2**20),
        name="blocks",
    )(coords, counts, adjacency, own, halo, cotangent)


def backward_kernel(
    remote, local, lists, x_ref, w_ref, in_grad, w_grad,
    landed, acc, gz, gz_rows, wpart, wland, pieces, pland, whole,
    nsend, nrecv, fsend, frecv, wsend, wrecv, psend, precv, asend, arecv,
):
    n = lax.axis_index("node")
    f = lax.axis_index("feat")
    barrier = enter(n, f)
    acc[...] = local[...]

    def add(p, vals):
        hot, hi = one_hot_t(lists, p)
        step = 8
        for g in range(0, GP, step):
            rows = jnp.concatenate(
                [jnp.where(hi == g + h, vals, 0.0).astype(jnp.bfloat16) for h in range(step)], axis=0
            )
            term = lax.dot_general(
                rows, hot, (((1,), (1,)), ((), ())), preferred_element_type=jnp.float32
            )
            acc[g : g + step] = acc[g : g + step] + term.reshape(step, CW, LO)

    pl.semaphore_wait(barrier, NN + NF - 2)

    def node_copy(k, to, source):
        return pltpu.make_async_remote_copy(
            src_ref=remote.at[to],
            dst_ref=landed.at[source],
            send_sem=nsend.at[k],
            recv_sem=nrecv.at[k],
            device_id={"node": to},
            device_id_type=MESH,
        )

    def start_node(k, c):
        node_copy(k, node_at(n, k), n).start()
        return c

    lax.fori_loop(1, NN, start_node, 0)
    add(n, remote[n].astype(jnp.float32))

    def take_node(k, c):
        source = node_back(n, k)
        node_copy(k, node_at(n, k), source).wait_recv()
        add(source, landed[source].astype(jnp.float32))
        return c

    lax.fori_loop(1, NN, take_node, 0)
    gz[...] = acc[...].astype(jnp.bfloat16)

    def feat_copy(k, to, source):
        return pltpu.make_async_remote_copy(
            src_ref=gz.at[pl.ds(to * GD, GD)],
            dst_ref=gz_rows.at[:, pl.ds(pl.multiple_of(source * CW, CW), CW), :],
            send_sem=fsend.at[k],
            recv_sem=frecv.at[k],
            device_id={"feat": to},
            device_id_type=MESH,
        )

    def start_feat(k, c):
        feat_copy(k, lax.rem(f + k, NF), f).start()
        return c

    lax.fori_loop(1, NF, start_feat, 0)
    gz_rows[:, pl.ds(pl.multiple_of(f * CW, CW), CW), :] = gz[pl.ds(f * GD, GD)]
    wt = w_ref[...].astype(jnp.float32).T.astype(jnp.bfloat16)

    def wait_feat(k, c):
        feat_copy(k, lax.rem(f + k, NF), lax.rem(f + NF - k, NF)).wait_recv()
        return c

    lax.fori_loop(1, NF, wait_feat, 0)

    total = jnp.zeros((F, F), jnp.float32)
    for h in range(GD):
        total = total + jnp.dot(
            gz_rows[h], x_ref[h * LO : (h + 1) * LO, :], preferred_element_type=jnp.float32
        )
    wpart[...] = total.reshape(NF, CW, F)

    def part_copy(k, to, source):
        return pltpu.make_async_remote_copy(
            src_ref=wpart.at[to],
            dst_ref=wland.at[source],
            send_sem=wsend.at[k],
            recv_sem=wrecv.at[k],
            device_id={"feat": to},
            device_id_type=MESH,
        )

    def start_part(k, c):
        part_copy(k, lax.rem(f + k, NF), f).start()
        return c

    lax.fori_loop(1, NF, start_part, 0)
    wland[f] = wpart[f]
    for h in range(GD):
        rows = gz_rows[h].astype(jnp.float32).T.astype(jnp.bfloat16)
        in_grad[h * LO : (h + 1) * LO, :] = jnp.dot(
            rows, wt, preferred_element_type=jnp.float32
        ).astype(jnp.bfloat16)

    def wait_part(k, c):
        part_copy(k, lax.rem(f + k, NF), lax.rem(f + NF - k, NF)).wait_recv()
        return c

    lax.fori_loop(1, NF, wait_part, 0)
    mine = wland[0]
    for g in range(1, NF):
        mine = mine + wland[g]
    mine = mine * (1.0 / math.sqrt(NN * ROWB * BLK))
    for i in range(CW):
        pieces[i] = mine[i : i + 1]

    def piece_copy(k, to, source):
        return pltpu.make_async_remote_copy(
            src_ref=pieces.at[to],
            dst_ref=pland.at[source],
            send_sem=psend.at[k],
            recv_sem=precv.at[k],
            device_id={"node": to},
            device_id_type=MESH,
        )

    def start_piece(k, c):
        piece_copy(k, node_at(n, k), n).start()
        return c

    lax.fori_loop(1, NN, start_piece, 0)
    pland[n] = pieces[n]

    def wait_piece(k, c):
        piece_copy(k, node_at(n, k), node_back(n, k)).wait_recv()
        return c

    lax.fori_loop(1, NN, wait_piece, 0)
    summed = pland[0]
    for i in range(1, NN):
        summed = summed + pland[i]
    whole[n] = summed

    def whole_copy(k, to, source):
        return pltpu.make_async_remote_copy(
            src_ref=whole.at[n],
            dst_ref=whole.at[source],
            send_sem=asend.at[k],
            recv_sem=arecv.at[k],
            device_id={"node": to},
            device_id_type=MESH,
        )

    def start_whole(k, c):
        whole_copy(k, node_at(n, k), n).start()
        return c

    lax.fori_loop(1, NN, start_whole, 0)

    def wait_whole(k, c):
        whole_copy(k, node_at(n, k), node_back(n, k)).wait_recv()
        return c

    lax.fori_loop(1, NN, wait_whole, 0)
    w_grad[...] = jnp.concatenate([whole[i] for i in range(CW)], axis=0).T

    def finish_node(k, c):
        node_copy(k, node_at(n, k), n).wait_send()
        piece_copy(k, node_at(n, k), n).wait_send()
        whole_copy(k, node_at(n, k), n).wait_send()
        return c

    lax.fori_loop(1, NN, finish_node, 0)

    def finish_feat(k, c):
        feat_copy(k, lax.rem(f + k, NF), f).wait_send()
        part_copy(k, lax.rem(f + k, NF), f).wait_send()
        return c

    lax.fori_loop(1, NF, finish_feat, 0)


def backward(remote, local, lists, features, weight):
    dma = pltpu.SemaphoreType.DMA
    return pl.pallas_call(
        backward_kernel,
        out_shape=(
            jax.ShapeDtypeStruct((RD, F), jnp.bfloat16),
            jax.ShapeDtypeStruct((F, CW), jnp.float32),
        ),
        in_specs=[pl.BlockSpec(memory_space=VMEM)] * 5,
        out_specs=(pl.BlockSpec(memory_space=VMEM),) * 2,
        scratch_shapes=[
            VMEM((NN, CW, HP), jnp.bfloat16),
            VMEM((GP, CW, LO), jnp.float32),
            VMEM((GP, CW, LO), jnp.bfloat16),
            VMEM((GD, F, LO), jnp.bfloat16),
            VMEM((NF, CW, F), jnp.float32),
            VMEM((NF, CW, F), jnp.float32),
            VMEM((NN, 1, F), jnp.float32),
            VMEM((NN, 1, F), jnp.float32),
            VMEM((NN, 1, F), jnp.float32),
            dma((NN,)),
            dma((NN,)),
            dma((NF,)),
            dma((NF,)),
            dma((NF,)),
            dma((NF,)),
            dma((NN,)),
            dma((NN,)),
            dma((NN,)),
            dma((NN,)),
        ],
        compiler_params=pltpu.CompilerParams(
            collective_id=1, has_side_effects=True, vmem_limit_bytes=32 * 2**20
        ),
        name="return_and_sum",
    )(remote, local, lists, features, weight)


def body(features, weight, adjacency, block_coords, block_counts, send_rows, cotangent):
    own, halo = forward(features, weight, send_rows)
    activations, local, remote = blocks(
        block_coords, block_counts, adjacency, own, halo, cotangent
    )
    input_grad, weight_grad = backward(remote, local, send_rows, features, weight)
    return (activations, input_grad, weight_grad)


def solution(mesh):
    return jax.shard_map(
        body,
        mesh=mesh,
        in_specs=(
            P(("node", "feat"), None),
            P(),
            P("node", None, None),
            P(None, "node"),
            P("node"),
            P("node", None),
            P("feat", "node"),
        ),
        out_specs=(P("feat", "node"), P(("node", "feat"), None), P(None, "feat")),
        check_vma=False,
    )
```

```python
import functools
import math

import jax
import jax.numpy as jnp
from jax import lax
from jax.experimental import pallas as pl
from jax.experimental.pallas import tpu as pltpu
from jax.sharding import PartitionSpec as P

ZS, XS = 8, 4
NN = ZS * XS
NF = 8
F = 256
CW = F // NF
RD = 1024
LO = 256
GD = RD // LO
GP = NF * GD
HP = 256
BLK = 128
ROWB = 64
COLB = 128
MAXB = 512
MESH = pl.DeviceIdType.MESH
VMEM = pltpu.VMEM


def node_at(n, k):
    z = ((n & -XS) + (k & -XS)) & (NN - 1)
    x = (n + k) & (XS - 1)
    return z + x


def node_back(n, k):
    z = ((n & -XS) + NN - (k & -XS)) & (NN - 1)
    x = (n + XS - (k & (XS - 1))) & (XS - 1)
    return z + x


def feat_at(f, k):
    return (f + k) & (NF - 1)


def feat_back(f, k):
    return (f + NF - k) & (NF - 1)


def enter(n, f):
    barrier = pltpu.get_barrier_semaphore()

    def greet_node(k, c):
        pl.semaphore_signal(barrier, inc=1, device_id={"node": node_at(n, k)}, device_id_type=MESH)
        return c

    def greet_feat(k, c):
        pl.semaphore_signal(barrier, inc=1, device_id={"feat": feat_at(f, k)}, device_id_type=MESH)
        return c

    lax.fori_loop(1, NF, greet_feat, 0)
    lax.fori_loop(1, NN, greet_node, 0)
    return barrier


def one_hot_t(lists, p):
    idx = lists[pl.ds(p, 1), :]
    lo = idx & (LO - 1)
    hi = lax.shift_right_logical(idx, 8)
    rows = lax.broadcasted_iota(jnp.int32, (LO, HP), 0)
    return (rows == lo).astype(jnp.float32).astype(jnp.bfloat16), hi


def forward_kernel(
    x_hbm, w_hbm, lists_hbm, adj_hbm, cot_hbm, coords_hbm,
    own, halo, adj, cot, coords,
    x_ref, w_ref, lists, proj, packed, fsend, frecv, nsend, nrecv, lsem,
):
    n = lax.axis_index("node")
    f = lax.axis_index("feat")
    loads = [
        pltpu.make_async_copy(src, dst, lsem.at[i])
        for i, (src, dst) in enumerate(
            [
                (x_hbm, x_ref),
                (w_hbm, w_ref),
                (lists_hbm, lists),
                (coords_hbm, coords),
                (cot_hbm, cot),
                (adj_hbm, adj),
            ]
        )
    ]
    for load in loads:
        load.start()
    barrier = enter(n, f)
    loads[0].wait()
    loads[1].wait()
    wt = w_ref[...].astype(jnp.float32).T.astype(jnp.bfloat16)
    for h in range(GD):
        proj[h] = lax.dot_general(
            wt,
            x_ref[h * LO : (h + 1) * LO, :],
            (((1,), (1,)), ((), ())),
            preferred_element_type=jnp.float32,
        ).astype(jnp.bfloat16)
    pl.semaphore_wait(barrier, NN + NF - 2)

    def feat_copy(k, to, source):
        return pltpu.make_async_remote_copy(
            src_ref=proj.at[:, pl.ds(pl.multiple_of(to * CW, CW), CW), :],
            dst_ref=own.at[pl.ds(source * GD, GD)],
            send_sem=fsend.at[k],
            recv_sem=frecv.at[k],
            device_id={"feat": to},
            device_id_type=MESH,
        )

    def start_feat(k, c):
        feat_copy(k, feat_at(f, k), f).start()
        return c

    lax.fori_loop(1, NF, start_feat, 0)
    loads[2].wait()
    own[pl.ds(f * GD, GD)] = proj[:, pl.ds(pl.multiple_of(f * CW, CW), CW), :]

    def wait_feat(k, c):
        feat_copy(k, feat_at(f, k), feat_back(f, k)).wait_recv()
        return c

    lax.fori_loop(1, NF, wait_feat, 0)

    def pick(p):
        hot, hi = one_hot_t(lists, p)
        got = jnp.zeros((CW, HP), jnp.float32)
        step = 8
        for g in range(0, GP, step):
            part = jnp.dot(
                own[g : g + step].reshape(step * CW, LO), hot, preferred_element_type=jnp.float32
            )
            for h in range(step):
                got = jnp.where(hi == g + h, part[h * CW : (h + 1) * CW], got)
        return got.astype(jnp.bfloat16)

    def node_copy(k, to, source):
        return pltpu.make_async_remote_copy(
            src_ref=packed.at[k],
            dst_ref=halo.at[source],
            send_sem=nsend.at[k],
            recv_sem=nrecv.at[k],
            device_id={"node": to},
            device_id_type=MESH,
        )

    def send_node(i, c):
        k = NN - i
        to = node_at(n, k)
        packed[k] = pick(to)
        node_copy(k, to, n).start()
        return c

    lax.fori_loop(1, NN, send_node, 0)
    halo[n] = pick(n)

    def finish_node(i, c):
        k = NN - i
        node_copy(k, node_at(n, k), node_back(n, k)).wait()
        return c

    lax.fori_loop(1, NN, finish_node, 0)

    def finish_feat(k, c):
        feat_copy(k, feat_at(f, k), f).wait_send()
        return c

    lax.fori_loop(1, NF, finish_feat, 0)
    for load in loads[3:]:
        load.wait()


def forward(features, weight, lists, adjacency, cotangent, coords):
    part = jax.ShapeDtypeStruct((GP, CW, LO), jnp.bfloat16)

    def like(a):
        return jax.ShapeDtypeStruct(a.shape, a.dtype)

    return pl.pallas_call(
        forward_kernel,
        out_shape=(part, part, like(adjacency), like(cotangent), like(coords)),
        in_specs=[pl.BlockSpec(memory_space=pltpu.HBM)] * 6,
        out_specs=(pl.BlockSpec(memory_space=VMEM),) * 5,
        scratch_shapes=[
            VMEM((RD, F), jnp.bfloat16),
            VMEM((F, F), jnp.bfloat16),
            VMEM((NN, HP), jnp.int32),
            VMEM((GD, F, LO), jnp.bfloat16),
            VMEM((NN, CW, HP), jnp.bfloat16),
            pltpu.SemaphoreType.DMA((NF,)),
            pltpu.SemaphoreType.DMA((NF,)),
            pltpu.SemaphoreType.DMA((NN,)),
            pltpu.SemaphoreType.DMA((NN,)),
            pltpu.SemaphoreType.DMA((6,)),
        ],
        compiler_params=pltpu.CompilerParams(
            collective_id=0, has_side_effects=True, vmem_limit_bytes=12 * 2**20
        ),
        name="project_and_send",
    )(
        *(
            pltpu.with_memory_space_constraint(a, pltpu.HBM)
            for a in (features, weight, lists, adjacency, cotangent, coords)
        )
    )


UNROLL = 32
NT = (((1,), (1,)), ((), ()))


def blocks_kernel(
    coords_v, counts, held, own, halo, cot, act, local, remote, coords, ext, pre, gpre, grad, sem
):
    load = pltpu.make_async_copy(coords_v, coords, sem)
    load.start()
    count = counts[0]
    pre[...] = jnp.zeros_like(pre)
    grad[...] = jnp.zeros_like(grad)
    for g in range(GP):
        for s in range(2):
            ext[2 * g + s] = own[g, :, s * BLK : (s + 1) * BLK]
            ext[ROWB + 2 * g + s] = halo[g, :, s * BLK : (s + 1) * BLK]
    load.wait()

    def row_of(b):
        return jnp.where(b < count, coords[0, b], ROWB)

    def gather(j, c):
        base = j * UNROLL
        terms = []
        for b in [base + u for u in range(0, UNROLL, 2)]:
            cols = jnp.concatenate([ext[coords[1, b]], ext[coords[1, b + 1]]], axis=0)
            pair = lax.dot_general(
                cols,
                held[pl.ds(b, 2)].reshape(2 * BLK, BLK),
                NT,
                preferred_element_type=jnp.float32,
            )
            terms += [pair[:CW, :BLK], pair[CW:, BLK:]]
        for u in range(UNROLL):
            r = row_of(base + u)
            pre[r] = pre[r] + terms[u]
        return c

    lax.fori_loop(0, MAXB // UNROLL, gather, 0)

    for r in range(ROWB):
        v = pre[r]
        at = slice(r * BLK, (r + 1) * BLK)
        sigma = jax.nn.sigmoid(v)
        act[:, at] = (v * sigma).astype(jnp.bfloat16)
        gpre[r] = (cot[:, at].astype(jnp.float32) * sigma * (1.0 + v * (1.0 - sigma))).astype(
            jnp.bfloat16
        )
    gpre[ROWB] = jnp.zeros((CW, BLK), jnp.bfloat16)

    def spread(j, c):
        base = j * UNROLL
        terms = []
        for b in [base + u for u in range(0, UNROLL, 2)]:
            rows = jnp.concatenate([gpre[row_of(b)], gpre[row_of(b + 1)]], axis=0)
            pair = jnp.dot(
                rows,
                jnp.concatenate([held[b], held[b + 1]], axis=1),
                preferred_element_type=jnp.float32,
            )
            terms += [pair[:CW, :BLK], pair[CW:, BLK:]]
        for u in range(UNROLL):
            col = coords[1, base + u]
            grad[col] = grad[col] + terms[u]
        return c

    lax.fori_loop(0, MAXB // UNROLL, spread, 0)
    for g in range(GP):
        for s in range(2):
            at = slice(s * BLK, (s + 1) * BLK)
            local[g, :, at] = grad[2 * g + s]
            remote[g, :, at] = grad[ROWB + 2 * g + s].astype(jnp.bfloat16)


def blocks(coords, counts, adjacency, own, halo, cotangent):
    return pl.pallas_call(
        blocks_kernel,
        out_shape=(
            jax.ShapeDtypeStruct((CW, ROWB * BLK), jnp.bfloat16),
            jax.ShapeDtypeStruct((GP, CW, LO), jnp.float32),
            jax.ShapeDtypeStruct((NN, CW, HP), jnp.bfloat16),
        ),
        in_specs=[
            pl.BlockSpec(memory_space=VMEM),
            pl.BlockSpec(memory_space=pltpu.SMEM),
            pl.BlockSpec(memory_space=VMEM),
            pl.BlockSpec(memory_space=VMEM),
            pl.BlockSpec(memory_space=VMEM),
            pl.BlockSpec(memory_space=VMEM),
        ],
        out_specs=(pl.BlockSpec(memory_space=VMEM),) * 3,
        scratch_shapes=[
            pltpu.SMEM((2, MAXB), jnp.int32),
            VMEM((COLB, CW, BLK), jnp.bfloat16),
            VMEM((ROWB + 1, CW, BLK), jnp.float32),
            VMEM((ROWB + 1, CW, BLK), jnp.bfloat16),
            VMEM((COLB, CW, BLK), jnp.float32),
            pltpu.SemaphoreType.DMA,
        ],
        compiler_params=pltpu.CompilerParams(vmem_limit_bytes=14 * 2**20),
        name="blocks",
    )(coords, counts, adjacency, own, halo, cotangent)


def backward_kernel(
    remote, local, lists, x_ref, w_ref, in_grad, w_grad,
    landed, acc, gz, gz_rows, wpart, wland, pieces, pland, zpart, zland, whole,
    nsend, nrecv, fsend, frecv, wsend, wrecv, psend, precv, zsend, zrecv, asend, arecv,
):
    n = lax.axis_index("node")
    f = lax.axis_index("feat")
    barrier = enter(n, f)
    acc[...] = local[...]

    def add(p, vals):
        hot, hi = one_hot_t(lists, p)
        step = 8
        for g in range(0, GP, step):
            rows = jnp.concatenate(
                [jnp.where(hi == g + h, vals, 0.0).astype(jnp.bfloat16) for h in range(step)], axis=0
            )
            term = lax.dot_general(
                rows, hot, (((1,), (1,)), ((), ())), preferred_element_type=jnp.float32
            )
            acc[g : g + step] = acc[g : g + step] + term.reshape(step, CW, LO)

    pl.semaphore_wait(barrier, NN + NF - 2)

    def node_copy(k, to, source):
        return pltpu.make_async_remote_copy(
            src_ref=remote.at[to],
            dst_ref=landed.at[source],
            send_sem=nsend.at[k],
            recv_sem=nrecv.at[k],
            device_id={"node": to},
            device_id_type=MESH,
        )

    def start_node(k, c):
        node_copy(k, node_at(n, k), n).start()
        return c

    lax.fori_loop(1, NN, start_node, 0)
    add(n, remote[n].astype(jnp.float32))

    def take_node(k, c):
        source = node_back(n, k)
        node_copy(k, node_at(n, k), source).wait_recv()
        add(source, landed[source].astype(jnp.float32))
        return c

    lax.fori_loop(1, NN, take_node, 0)
    gz[...] = acc[...].astype(jnp.bfloat16)

    def feat_copy(k, to, source):
        return pltpu.make_async_remote_copy(
            src_ref=gz.at[pl.ds(to * GD, GD)],
            dst_ref=gz_rows.at[:, pl.ds(pl.multiple_of(source * CW, CW), CW), :],
            send_sem=fsend.at[k],
            recv_sem=frecv.at[k],
            device_id={"feat": to},
            device_id_type=MESH,
        )

    def start_feat(k, c):
        feat_copy(k, feat_at(f, k), f).start()
        return c

    lax.fori_loop(1, NF, start_feat, 0)
    gz_rows[:, pl.ds(pl.multiple_of(f * CW, CW), CW), :] = gz[pl.ds(f * GD, GD)]
    wt = w_ref[...].astype(jnp.float32).T.astype(jnp.bfloat16)

    def wait_feat(k, c):
        feat_copy(k, feat_at(f, k), feat_back(f, k)).wait_recv()
        return c

    lax.fori_loop(1, NF, wait_feat, 0)

    total = jnp.zeros((F, F), jnp.float32)
    for h in range(GD):
        total = total + jnp.dot(
            gz_rows[h], x_ref[h * LO : (h + 1) * LO, :], preferred_element_type=jnp.float32
        )
    wpart[...] = total.reshape(NF, CW, F)

    def part_copy(k, to, source):
        return pltpu.make_async_remote_copy(
            src_ref=wpart.at[to],
            dst_ref=wland.at[source],
            send_sem=wsend.at[k],
            recv_sem=wrecv.at[k],
            device_id={"feat": to},
            device_id_type=MESH,
        )

    def start_part(k, c):
        part_copy(k, feat_at(f, k), f).start()
        return c

    lax.fori_loop(1, NF, start_part, 0)
    wland[f] = wpart[f]
    for h in range(GD):
        rows = gz_rows[h].astype(jnp.float32).T.astype(jnp.bfloat16)
        in_grad[h * LO : (h + 1) * LO, :] = jnp.dot(
            rows, wt, preferred_element_type=jnp.float32
        ).astype(jnp.bfloat16)

    def wait_part(k, c):
        part_copy(k, feat_at(f, k), feat_back(f, k)).wait_recv()
        return c

    lax.fori_loop(1, NF, wait_part, 0)
    mine = wland[0]
    for g in range(1, NF):
        mine = mine + wland[g]
    mine = mine * (1.0 / math.sqrt(NN * ROWB * BLK))
    z, x = n & -XS, n & (XS - 1)
    pieces[...] = mine.reshape(XS, CW // XS, F)

    def x_at(k):
        return z + ((x + k) & (XS - 1))

    def z_at(k):
        return ((z + XS * k) & (NN - 1)) + x

    def share_copy(k, source):
        to = x_at(k)
        return pltpu.make_async_remote_copy(
            src_ref=pieces.at[to & (XS - 1)],
            dst_ref=pland.at[source & (XS - 1)],
            send_sem=psend.at[k],
            recv_sem=precv.at[k],
            device_id={"node": to},
            device_id_type=MESH,
        )

    for k in range(1, XS):
        share_copy(k, n).start()
    pland[x] = pieces[x]
    for k in range(1, XS):
        share_copy(k, x_at(XS - k)).wait_recv()
    zpart[...] = pland[0] + pland[1] + pland[2] + pland[3]

    def z_copy(k, source):
        return pltpu.make_async_remote_copy(
            src_ref=zpart,
            dst_ref=zland.at[lax.shift_right_logical(source, 2)],
            send_sem=zsend.at[k],
            recv_sem=zrecv.at[k],
            device_id={"node": z_at(k)},
            device_id_type=MESH,
        )

    for k in range(1, ZS):
        z_copy(k, n).start()
    zland[lax.shift_right_logical(n, 2)] = zpart[...]
    for k in range(1, ZS):
        z_copy(k, z_at(ZS - k)).wait_recv()
    summed = zland[0]
    for i in range(1, ZS):
        summed = summed + zland[i]
    whole[x] = summed

    def back_copy(k, source):
        return pltpu.make_async_remote_copy(
            src_ref=whole.at[x],
            dst_ref=whole.at[source & (XS - 1)],
            send_sem=asend.at[k],
            recv_sem=arecv.at[k],
            device_id={"node": x_at(k)},
            device_id_type=MESH,
        )

    for k in range(1, XS):
        back_copy(k, n).start()
    for k in range(1, XS):
        back_copy(k, x_at(XS - k)).wait_recv()
    w_grad[...] = whole[...].reshape(CW, F)
    for k in range(1, XS):
        share_copy(k, n).wait_send()
        back_copy(k, n).wait_send()
    for k in range(1, ZS):
        z_copy(k, n).wait_send()

    def finish_node(k, c):
        node_copy(k, node_at(n, k), n).wait_send()
        return c

    lax.fori_loop(1, NN, finish_node, 0)

    def finish_feat(k, c):
        feat_copy(k, feat_at(f, k), f).wait_send()
        part_copy(k, feat_at(f, k), f).wait_send()
        return c

    lax.fori_loop(1, NF, finish_feat, 0)


def backward(remote, local, lists, features, weight):
    dma = pltpu.SemaphoreType.DMA
    return pl.pallas_call(
        backward_kernel,
        out_shape=(
            jax.ShapeDtypeStruct((RD, F), jnp.bfloat16),
            jax.ShapeDtypeStruct((CW, F), jnp.float32),
        ),
        in_specs=[pl.BlockSpec(memory_space=VMEM)] * 5,
        out_specs=(pl.BlockSpec(memory_space=VMEM),) * 2,
        scratch_shapes=[
            VMEM((NN, CW, HP), jnp.bfloat16),
            VMEM((GP, CW, LO), jnp.float32),
            VMEM((GP, CW, LO), jnp.bfloat16),
            VMEM((GD, F, LO), jnp.bfloat16),
            VMEM((NF, CW, F), jnp.float32),
            VMEM((NF, CW, F), jnp.float32),
            VMEM((XS, CW // XS, F), jnp.float32),
            VMEM((XS, CW // XS, F), jnp.float32),
            VMEM((CW // XS, F), jnp.float32),
            VMEM((ZS, CW // XS, F), jnp.float32),
            VMEM((XS, CW // XS, F), jnp.float32),
            dma((NN,)),
            dma((NN,)),
            dma((NF,)),
            dma((NF,)),
            dma((NF,)),
            dma((NF,)),
            dma((XS,)),
            dma((XS,)),
            dma((ZS,)),
            dma((ZS,)),
            dma((XS,)),
            dma((XS,)),
        ],
        compiler_params=pltpu.CompilerParams(
            collective_id=1, has_side_effects=True, vmem_limit_bytes=32 * 2**20
        ),
        name="return_and_sum",
    )(remote, local, lists, features, weight)


def body(features, weight, adjacency, block_coords, block_counts, send_rows, cotangent):
    own, halo, held, cot, coords = forward(
        features, weight, send_rows, adjacency, cotangent, block_coords
    )
    activations, local, remote = blocks(coords, block_counts, held, own, halo, cot)
    input_grad, weight_grad_t = backward(remote, local, send_rows, features, weight)
    weight_grad = weight_grad_t.T
    return (activations, input_grad, weight_grad)


def solution(mesh):
    return jax.shard_map(
        body,
        mesh=mesh,
        in_specs=(
            P(("node", "feat"), None),
            P(),
            P("node", None, None),
            P(None, "node"),
            P("node"),
            P("node", None),
            P("feat", "node"),
        ),
        out_specs=(P("feat", "node"), P(("node", "feat"), None), P(None, "feat")),
        check_vma=False,
    )
```

```python
import functools
import math

import jax
import jax.numpy as jnp
from jax import lax
from jax.experimental import pallas as pl
from jax.experimental.pallas import tpu as pltpu
from jax.sharding import PartitionSpec as P

ZS, XS = 8, 4
NN = ZS * XS
NF = 8
NY = 4
F = 256
CW = F // NF
RD = 1024
LO = 256
GD = RD // LO
GP = NF * GD
HP = 256
BLK = 128
ROWB = 64
COLB = 128
MAXB = 512
MESH = pl.DeviceIdType.MESH
VMEM = pltpu.VMEM


def node_at(n, k):
    z = ((n & -XS) + (k & -XS)) & (NN - 1)
    x = (n + k) & (XS - 1)
    return z + x


def node_back(n, k):
    z = ((n & -XS) + NN - (k & -XS)) & (NN - 1)
    x = (n + XS - (k & (XS - 1))) & (XS - 1)
    return z + x


def feat_at(f, k):
    return (f + k) & (NF - 1)


def feat_back(f, k):
    return (f + NF - k) & (NF - 1)


def enter(n, f):
    barrier = pltpu.get_barrier_semaphore()

    def greet_node(k, c):
        pl.semaphore_signal(barrier, inc=1, device_id={"node": node_at(n, k)}, device_id_type=MESH)
        return c

    def greet_feat(k, c):
        pl.semaphore_signal(barrier, inc=1, device_id={"feat": feat_at(f, k)}, device_id_type=MESH)
        return c

    lax.fori_loop(1, NF, greet_feat, 0)
    lax.fori_loop(1, NN, greet_node, 0)
    return barrier


def one_hot_t(lists, p):
    idx = lists[pl.ds(p, 1), :]
    lo = idx & (LO - 1)
    hi = lax.shift_right_logical(idx, 8)
    rows = lax.broadcasted_iota(jnp.int32, (LO, HP), 0)
    return (rows == lo).astype(jnp.float32).astype(jnp.bfloat16), hi


def forward_kernel(
    x_hbm, w_hbm, lists_hbm, adj_hbm, cot_hbm, coords_hbm,
    own, halo, xs, adj, cot, coords,
    w_ref, lists, proj, packed, fsend, frecv, nsend, nrecv, xsend, xrecv, lsem,
):
    n = lax.axis_index("node")
    f = lax.axis_index("feat")
    y = lax.shift_right_logical(f, 1)
    x_ref = xs.at[y]
    loads = [
        pltpu.make_async_copy(src, dst, lsem.at[i])
        for i, (src, dst) in enumerate(
            [
                (x_hbm, x_ref),
                (w_hbm, w_ref),
                (lists_hbm, lists),
                (coords_hbm, coords),
                (cot_hbm, cot),
                (adj_hbm, adj),
            ]
        )
    ]
    for load in loads:
        load.start()
    barrier = enter(n, f)
    loads[0].wait()
    loads[1].wait()
    wt = w_ref[...].astype(jnp.float32).T.astype(jnp.bfloat16)
    for h in range(GD):
        proj[h] = lax.dot_general(
            wt,
            xs[y, h * LO : (h + 1) * LO, :],
            (((1,), (1,)), ((), ())),
            preferred_element_type=jnp.float32,
        ).astype(jnp.bfloat16)
    pl.semaphore_wait(barrier, NN + NF - 2)

    def feat_copy(k, to, source):
        return pltpu.make_async_remote_copy(
            src_ref=proj.at[:, pl.ds(pl.multiple_of(to * CW, CW), CW), :],
            dst_ref=own.at[pl.ds(source * GD, GD)],
            send_sem=fsend.at[k],
            recv_sem=frecv.at[k],
            device_id={"feat": to},
            device_id_type=MESH,
        )

    def start_feat(k, c):
        feat_copy(k, feat_at(f, k), f).start()
        return c

    lax.fori_loop(1, NF, start_feat, 0)
    loads[2].wait()
    own[pl.ds(f * GD, GD)] = proj[:, pl.ds(pl.multiple_of(f * CW, CW), CW), :]

    def wait_feat(k, c):
        feat_copy(k, feat_at(f, k), feat_back(f, k)).wait_recv()
        return c

    lax.fori_loop(1, NF, wait_feat, 0)

    def rows_copy(k, source):
        return pltpu.make_async_remote_copy(
            src_ref=xs.at[y],
            dst_ref=xs.at[source],
            send_sem=xsend.at[k],
            recv_sem=xrecv.at[k],
            device_id={"feat": feat_at(f, 2 * k)},
            device_id_type=MESH,
        )

    for k in (1, 3):
        rows_copy(k, y).start()

    def pick(p):
        hot, hi = one_hot_t(lists, p)
        got = jnp.zeros((CW, HP), jnp.float32)
        step = 8
        for g in range(0, GP, step):
            part = jnp.dot(
                own[g : g + step].reshape(step * CW, LO), hot, preferred_element_type=jnp.float32
            )
            for h in range(step):
                got = jnp.where(hi == g + h, part[h * CW : (h + 1) * CW], got)
        return got.astype(jnp.bfloat16)

    def node_copy(k, to, source):
        return pltpu.make_async_remote_copy(
            src_ref=packed.at[k],
            dst_ref=halo.at[source],
            send_sem=nsend.at[k],
            recv_sem=nrecv.at[k],
            device_id={"node": to},
            device_id_type=MESH,
        )

    def send_node(i, c):
        k = NN - i
        to = node_at(n, k)
        packed[k] = pick(to)
        node_copy(k, to, n).start()
        return c

    lax.fori_loop(1, NN, send_node, 0)
    halo[n] = pick(n)

    def finish_node(i, c):
        k = NN - i
        node_copy(k, node_at(n, k), node_back(n, k)).wait()
        return c

    lax.fori_loop(1, NN, finish_node, 0)

    def finish_feat(k, c):
        feat_copy(k, feat_at(f, k), f).wait_send()
        return c

    lax.fori_loop(1, NF, finish_feat, 0)
    for k in (1, 3):
        rows_copy(k, (y + NY - k) & (NY - 1)).wait()
    for load in loads[3:]:
        load.wait()


def forward(features, weight, lists, adjacency, cotangent, coords):
    part = jax.ShapeDtypeStruct((GP, CW, LO), jnp.bfloat16)

    def like(a):
        return jax.ShapeDtypeStruct(a.shape, a.dtype)

    return pl.pallas_call(
        forward_kernel,
        out_shape=(
            part,
            part,
            jax.ShapeDtypeStruct((NY, RD, F), jnp.bfloat16),
            like(adjacency),
            like(cotangent),
            like(coords),
        ),
        in_specs=[pl.BlockSpec(memory_space=pltpu.HBM)] * 6,
        out_specs=(pl.BlockSpec(memory_space=VMEM),) * 6,
        scratch_shapes=[
            VMEM((F, F), jnp.bfloat16),
            VMEM((NN, HP), jnp.int32),
            VMEM((GD, F, LO), jnp.bfloat16),
            VMEM((NN, CW, HP), jnp.bfloat16),
            pltpu.SemaphoreType.DMA((NF,)),
            pltpu.SemaphoreType.DMA((NF,)),
            pltpu.SemaphoreType.DMA((NN,)),
            pltpu.SemaphoreType.DMA((NN,)),
            pltpu.SemaphoreType.DMA((NY,)),
            pltpu.SemaphoreType.DMA((NY,)),
            pltpu.SemaphoreType.DMA((6,)),
        ],
        compiler_params=pltpu.CompilerParams(
            collective_id=0, has_side_effects=True, vmem_limit_bytes=12 * 2**20
        ),
        name="project_and_send",
    )(
        *(
            pltpu.with_memory_space_constraint(a, pltpu.HBM)
            for a in (features, weight, lists, adjacency, cotangent, coords)
        )
    )


UNROLL = 32
NT = (((1,), (1,)), ((), ()))


def blocks_kernel(
    coords_v, counts, held, own, halo, cot, act, local, remote, coords, ext, pre, gpre, grad, sem
):
    load = pltpu.make_async_copy(coords_v, coords, sem)
    load.start()
    count = counts[0]
    pre[...] = jnp.zeros_like(pre)
    grad[...] = jnp.zeros_like(grad)
    for g in range(GP):
        for s in range(2):
            ext[2 * g + s] = own[g, :, s * BLK : (s + 1) * BLK]
            ext[ROWB + 2 * g + s] = halo[g, :, s * BLK : (s + 1) * BLK]
    load.wait()

    def row_of(b):
        return jnp.where(b < count, coords[0, b], ROWB)

    def gather(j, c):
        base = j * UNROLL
        terms = []
        for b in [base + u for u in range(0, UNROLL, 2)]:
            cols = jnp.concatenate([ext[coords[1, b]], ext[coords[1, b + 1]]], axis=0)
            pair = lax.dot_general(
                cols,
                held[pl.ds(b, 2)].reshape(2 * BLK, BLK),
                NT,
                preferred_element_type=jnp.float32,
            )
            terms += [pair[:CW, :BLK], pair[CW:, BLK:]]
        for u in range(UNROLL):
            r = row_of(base + u)
            pre[r] = pre[r] + terms[u]
        return c

    lax.fori_loop(0, MAXB // UNROLL, gather, 0)

    for r in range(ROWB):
        v = pre[r]
        at = slice(r * BLK, (r + 1) * BLK)
        sigma = jax.nn.sigmoid(v)
        act[:, at] = (v * sigma).astype(jnp.bfloat16)
        gpre[r] = (cot[:, at].astype(jnp.float32) * sigma * (1.0 + v * (1.0 - sigma))).astype(
            jnp.bfloat16
        )
    gpre[ROWB] = jnp.zeros((CW, BLK), jnp.bfloat16)

    def spread(j, c):
        base = j * UNROLL
        terms = []
        for b in [base + u for u in range(0, UNROLL, 2)]:
            rows = jnp.concatenate([gpre[row_of(b)], gpre[row_of(b + 1)]], axis=0)
            pair = jnp.dot(
                rows,
                jnp.concatenate([held[b], held[b + 1]], axis=1),
                preferred_element_type=jnp.float32,
            )
            terms += [pair[:CW, :BLK], pair[CW:, BLK:]]
        for u in range(UNROLL):
            col = coords[1, base + u]
            grad[col] = grad[col] + terms[u]
        return c

    lax.fori_loop(0, MAXB // UNROLL, spread, 0)
    for g in range(GP):
        for s in range(2):
            at = slice(s * BLK, (s + 1) * BLK)
            local[g, :, at] = grad[2 * g + s]
            remote[g, :, at] = grad[ROWB + 2 * g + s].astype(jnp.bfloat16)


def blocks(coords, counts, adjacency, own, halo, cotangent):
    return pl.pallas_call(
        blocks_kernel,
        out_shape=(
            jax.ShapeDtypeStruct((CW, ROWB * BLK), jnp.bfloat16),
            jax.ShapeDtypeStruct((GP, CW, LO), jnp.float32),
            jax.ShapeDtypeStruct((NN, CW, HP), jnp.bfloat16),
        ),
        in_specs=[
            pl.BlockSpec(memory_space=VMEM),
            pl.BlockSpec(memory_space=pltpu.SMEM),
            pl.BlockSpec(memory_space=VMEM),
            pl.BlockSpec(memory_space=VMEM),
            pl.BlockSpec(memory_space=VMEM),
            pl.BlockSpec(memory_space=VMEM),
        ],
        out_specs=(pl.BlockSpec(memory_space=VMEM),) * 3,
        scratch_shapes=[
            pltpu.SMEM((2, MAXB), jnp.int32),
            VMEM((COLB, CW, BLK), jnp.bfloat16),
            VMEM((ROWB + 1, CW, BLK), jnp.float32),
            VMEM((ROWB + 1, CW, BLK), jnp.bfloat16),
            VMEM((COLB, CW, BLK), jnp.float32),
            pltpu.SemaphoreType.DMA,
        ],
        compiler_params=pltpu.CompilerParams(vmem_limit_bytes=14 * 2**20),
        name="blocks",
    )(coords, counts, adjacency, own, halo, cotangent)


def backward_kernel(
    remote, local, lists, xs, w_ref, in_grad, w_grad,
    x_far, x_other, landed, acc, gz, gz_rows, pieces, pland, zpart, zland, whole,
    nsend, nrecv, fsend, frecv, xsend, xrecv, osend, orecv, psend, precv, zsend, zrecv, asend, arecv,
):
    n = lax.axis_index("node")
    f = lax.axis_index("feat")
    y = lax.shift_right_logical(f, 1)
    core = f & 1
    far = y ^ 2
    barrier = enter(n, f)
    acc[...] = local[...]

    def add(p, vals):
        hot, hi = one_hot_t(lists, p)
        step = 8
        for g in range(0, GP, step):
            rows = jnp.concatenate(
                [jnp.where(hi == g + h, vals, 0.0).astype(jnp.bfloat16) for h in range(step)], axis=0
            )
            term = lax.dot_general(
                rows, hot, (((1,), (1,)), ((), ())), preferred_element_type=jnp.float32
            )
            acc[g : g + step] = acc[g : g + step] + term.reshape(step, CW, LO)

    pl.semaphore_wait(barrier, NN + NF - 2)

    def node_copy(k, to, source):
        return pltpu.make_async_remote_copy(
            src_ref=remote.at[to],
            dst_ref=landed.at[source],
            send_sem=nsend.at[k],
            recv_sem=nrecv.at[k],
            device_id={"node": to},
            device_id_type=MESH,
        )

    def start_node(k, c):
        node_copy(k, node_at(n, k), n).start()
        return c

    lax.fori_loop(1, NN, start_node, 0)
    far_copy = pltpu.make_async_remote_copy(
        src_ref=xs.at[y],
        dst_ref=x_far,
        send_sem=xsend,
        recv_sem=xrecv,
        device_id={"feat": f ^ 4},
        device_id_type=MESH,
    )

    def other_copy(k, src):
        return pltpu.make_async_remote_copy(
            src_ref=src,
            dst_ref=x_other.at[(y + k) & (NY - 1)],
            send_sem=osend.at[k],
            recv_sem=orecv.at[k],
            device_id={"feat": f ^ 1},
            device_id_type=MESH,
        )

    far_copy.start()
    for k in (0, 1, 3):
        other_copy(k, xs.at[(y + k) & (NY - 1)]).start()
    add(n, remote[n].astype(jnp.float32))

    def take_node(k, c):
        source = node_back(n, k)
        node_copy(k, node_at(n, k), source).wait_recv()
        add(source, landed[source].astype(jnp.float32))
        return c

    lax.fori_loop(1, NN - 6, take_node, 0)
    far_copy.wait_recv()
    other_copy(2, x_far).start()
    lax.fori_loop(NN - 6, NN, take_node, 0)
    gz[...] = acc[...].astype(jnp.bfloat16)

    def feat_copy(k, to, source):
        return pltpu.make_async_remote_copy(
            src_ref=gz.at[pl.ds(to * GD, GD)],
            dst_ref=gz_rows.at[:, pl.ds(pl.multiple_of(source * CW, CW), CW), :],
            send_sem=fsend.at[k],
            recv_sem=frecv.at[k],
            device_id={"feat": to},
            device_id_type=MESH,
        )

    def start_feat(k, c):
        feat_copy(k, feat_at(f, k), f).start()
        return c

    lax.fori_loop(1, NF, start_feat, 0)
    for k in range(NY):
        other_copy(k, x_far).wait_recv()

    def product(rows, at, group):
        out = jnp.zeros((CW, F), jnp.float32)
        for j in range(GD):
            out = out + jnp.dot(
                gz[group + j],
                rows[at, j * LO : (j + 1) * LO, :],
                preferred_element_type=jnp.float32,
            )
        return out

    mine = product(x_far.reshape(1, RD, F), 0, GD * (2 * far + core))
    for k in (0, 1, 3):
        at = (y + k) & (NY - 1)
        mine = mine + product(xs, at, GD * (2 * at + core))
    for at in range(NY):
        mine = mine + product(x_other, at, GD * (2 * at + 1 - core))
    mine = mine * (1.0 / math.sqrt(NN * ROWB * BLK))
    z, x = n & -XS, n & (XS - 1)
    pieces[...] = mine.reshape(XS, CW // XS, F)

    def x_at(k):
        return z + ((x + k) & (XS - 1))

    def z_at(k):
        return ((z + XS * k) & (NN - 1)) + x

    def share_copy(k, source):
        to = x_at(k)
        return pltpu.make_async_remote_copy(
            src_ref=pieces.at[to & (XS - 1)],
            dst_ref=pland.at[source & (XS - 1)],
            send_sem=psend.at[k],
            recv_sem=precv.at[k],
            device_id={"node": to},
            device_id_type=MESH,
        )

    for k in range(1, XS):
        share_copy(k, n).start()
    pland[x] = pieces[x]
    for k in range(1, XS):
        share_copy(k, x_at(XS - k)).wait_recv()
    zpart[...] = pland[0] + pland[1] + pland[2] + pland[3]

    def z_copy(k, source):
        return pltpu.make_async_remote_copy(
            src_ref=zpart,
            dst_ref=zland.at[lax.shift_right_logical(source, 2)],
            send_sem=zsend.at[k],
            recv_sem=zrecv.at[k],
            device_id={"node": z_at(k)},
            device_id_type=MESH,
        )

    for k in range(1, ZS):
        z_copy(k, n).start()

    gz_rows[:, pl.ds(pl.multiple_of(f * CW, CW), CW), :] = gz[pl.ds(f * GD, GD)]
    wt = w_ref[...].astype(jnp.float32).T.astype(jnp.bfloat16)

    def wait_feat(k, c):
        feat_copy(k, feat_at(f, k), feat_back(f, k)).wait_recv()
        return c

    lax.fori_loop(1, NF, wait_feat, 0)
    for h in range(GD):
        rows = gz_rows[h].astype(jnp.float32).T.astype(jnp.bfloat16)
        in_grad[h * LO : (h + 1) * LO, :] = jnp.dot(
            rows, wt, preferred_element_type=jnp.float32
        ).astype(jnp.bfloat16)

    zland[lax.shift_right_logical(n, 2)] = zpart[...]
    for k in range(1, ZS):
        z_copy(k, z_at(ZS - k)).wait_recv()
    summed = zland[0]
    for i in range(1, ZS):
        summed = summed + zland[i]
    whole[x] = summed

    def back_copy(k, source):
        return pltpu.make_async_remote_copy(
            src_ref=whole.at[x],
            dst_ref=whole.at[source & (XS - 1)],
            send_sem=asend.at[k],
            recv_sem=arecv.at[k],
            device_id={"node": x_at(k)},
            device_id_type=MESH,
        )

    for k in range(1, XS):
        back_copy(k, n).start()
    for k in range(1, XS):
        back_copy(k, x_at(XS - k)).wait_recv()
    w_grad[...] = whole[...].reshape(CW, F)
    for k in range(1, XS):
        share_copy(k, n).wait_send()
        back_copy(k, n).wait_send()
    for k in range(1, ZS):
        z_copy(k, n).wait_send()

    def finish_node(k, c):
        node_copy(k, node_at(n, k), n).wait_send()
        return c

    lax.fori_loop(1, NN, finish_node, 0)

    def finish_feat(k, c):
        feat_copy(k, feat_at(f, k), f).wait_send()
        return c

    lax.fori_loop(1, NF, finish_feat, 0)
    far_copy.wait_send()
    for k in range(NY):
        other_copy(k, x_far).wait_send()


def backward(remote, local, lists, xs, weight):
    dma = pltpu.SemaphoreType.DMA
    return pl.pallas_call(
        backward_kernel,
        out_shape=(
            jax.ShapeDtypeStruct((RD, F), jnp.bfloat16),
            jax.ShapeDtypeStruct((CW, F), jnp.float32),
        ),
        in_specs=[
            pl.BlockSpec(memory_space=VMEM),
            pl.BlockSpec(memory_space=VMEM),
            pl.BlockSpec(memory_space=VMEM),
            pl.BlockSpec(memory_space=VMEM),
            pl.BlockSpec(memory_space=VMEM),
        ],
        out_specs=(pl.BlockSpec(memory_space=VMEM),) * 2,
        scratch_shapes=[
            VMEM((RD, F), jnp.bfloat16),
            VMEM((NY, RD, F), jnp.bfloat16),
            VMEM((NN, CW, HP), jnp.bfloat16),
            VMEM((GP, CW, LO), jnp.float32),
            VMEM((GP, CW, LO), jnp.bfloat16),
            VMEM((GD, F, LO), jnp.bfloat16),
            VMEM((XS, CW // XS, F), jnp.float32),
            VMEM((XS, CW // XS, F), jnp.float32),
            VMEM((CW // XS, F), jnp.float32),
            VMEM((ZS, CW // XS, F), jnp.float32),
            VMEM((XS, CW // XS, F), jnp.float32),
            dma((NN,)),
            dma((NN,)),
            dma((NF,)),
            dma((NF,)),
            dma,
            dma,
            dma((NY,)),
            dma((NY,)),
            dma((XS,)),
            dma((XS,)),
            dma((ZS,)),
            dma((ZS,)),
            dma((XS,)),
            dma((XS,)),
        ],
        compiler_params=pltpu.CompilerParams(
            collective_id=1, has_side_effects=True, vmem_limit_bytes=32 * 2**20
        ),
        name="return_and_sum",
    )(remote, local, lists, xs, weight)


def body(features, weight, adjacency, block_coords, block_counts, send_rows, cotangent):
    own, halo, xs, held, cot, coords = forward(
        features, weight, send_rows, adjacency, cotangent, block_coords
    )
    activations, local, remote = blocks(coords, block_counts, held, own, halo, cot)
    input_grad, weight_grad_t = backward(remote, local, send_rows, xs, weight)
    weight_grad = weight_grad_t.T
    return (activations, input_grad, weight_grad)


def solution(mesh):
    return jax.shard_map(
        body,
        mesh=mesh,
        in_specs=(
            P(("node", "feat"), None),
            P(),
            P("node", None, None),
            P(None, "node"),
            P("node"),
            P("node", None),
            P("feat", "node"),
        ),
        out_specs=(P("feat", "node"), P(("node", "feat"), None), P(None, "feat")),
        check_vma=False,
    )
```

```python
import functools
import math

import jax
import jax.numpy as jnp
from jax import lax
from jax.experimental import pallas as pl
from jax.experimental.pallas import tpu as pltpu
from jax.sharding import PartitionSpec as P

ZS, XS = 8, 4
NN = ZS * XS
NF = 8
NY = 4
F = 256
CW = F // NF
RD = 1024
LO = 256
GD = RD // LO
GP = NF * GD
HP = 256
BLK = 128
NT = (((1,), (1,)), ((), ()))
ROWB = 64
COLB = 128
MAXB = 512
MESH = pl.DeviceIdType.MESH
VMEM = pltpu.VMEM


def node_at(n, k):
    z = ((n & -XS) + (k & -XS)) & (NN - 1)
    x = (n + k) & (XS - 1)
    return z + x


def node_back(n, k):
    z = ((n & -XS) + NN - (k & -XS)) & (NN - 1)
    x = (n + XS - (k & (XS - 1))) & (XS - 1)
    return z + x


def far_first(i):
    return ZS // 2 + (i // 2) * (1 - (i & 1)) - ((i + 1) // 2) * (i & 1)


def feat_at(f, k):
    return (f + k) & (NF - 1)


def feat_back(f, k):
    return (f + NF - k) & (NF - 1)


def enter(n, f):
    barrier = pltpu.get_barrier_semaphore()

    def greet_node(k, c):
        pl.semaphore_signal(barrier, inc=1, device_id={"node": node_at(n, k)}, device_id_type=MESH)
        return c

    def greet_feat(k, c):
        pl.semaphore_signal(barrier, inc=1, device_id={"feat": feat_at(f, k)}, device_id_type=MESH)
        return c

    lax.fori_loop(1, NF, greet_feat, 0)
    lax.fori_loop(1, NN, greet_node, 0)
    return barrier


def one_hot_t(lists, p):
    idx = lists[pl.ds(p, 1), :]
    lo = idx & (LO - 1)
    hi = lax.shift_right_logical(idx, 8)
    rows = lax.broadcasted_iota(jnp.int32, (LO, HP), 0)
    return (rows == lo).astype(jnp.float32).astype(jnp.bfloat16), hi


def forward_kernel(
    x_hbm, w_hbm, lists_hbm, adj_hbm, cot_hbm, coords_hbm,
    own, halo, xs, adj, cot, coords,
    w_ref, lists, proj, packed, fsend, frecv, nsend, nrecv, xsend, xrecv, lsem,
):
    n = lax.axis_index("node")
    f = lax.axis_index("feat")
    y = lax.shift_right_logical(f, 1)
    x_ref = xs.at[y]
    loads = [
        pltpu.make_async_copy(src, dst, lsem.at[i])
        for i, (src, dst) in enumerate(
            [
                (x_hbm, x_ref),
                (w_hbm, w_ref),
                (lists_hbm, lists),
                (coords_hbm, coords),
                (cot_hbm, cot),
                (adj_hbm, adj),
            ]
        )
    ]
    for load in loads:
        load.start()
    barrier = enter(n, f)
    loads[0].wait()
    loads[1].wait()
    wt = w_ref[...].astype(jnp.float32).T.astype(jnp.bfloat16)
    for h in range(GD):
        proj[h] = lax.dot_general(
            wt,
            xs[y, h * LO : (h + 1) * LO, :],
            (((1,), (1,)), ((), ())),
            preferred_element_type=jnp.float32,
        ).astype(jnp.bfloat16)
    pl.semaphore_wait(barrier, NN + NF - 2)

    def feat_copy(k, to, source):
        return pltpu.make_async_remote_copy(
            src_ref=proj.at[:, pl.ds(pl.multiple_of(to * CW, CW), CW), :],
            dst_ref=own.at[pl.ds(source * GD, GD)],
            send_sem=fsend.at[k],
            recv_sem=frecv.at[k],
            device_id={"feat": to},
            device_id_type=MESH,
        )

    def start_feat(k, c):
        feat_copy(k, feat_at(f, k), f).start()
        return c

    lax.fori_loop(1, NF, start_feat, 0)
    loads[2].wait()
    own[pl.ds(f * GD, GD)] = proj[:, pl.ds(pl.multiple_of(f * CW, CW), CW), :]

    def wait_feat(k, c):
        feat_copy(k, feat_at(f, k), feat_back(f, k)).wait_recv()
        return c

    lax.fori_loop(1, NF, wait_feat, 0)

    def rows_copy(k, source):
        return pltpu.make_async_remote_copy(
            src_ref=xs.at[y],
            dst_ref=xs.at[source],
            send_sem=xsend.at[k],
            recv_sem=xrecv.at[k],
            device_id={"feat": feat_at(f, 2 * k)},
            device_id_type=MESH,
        )

    for k in (1, 3):
        rows_copy(k, y).start()

    def pick(lists_at):
        hots = [one_hot_t(lists, p) for p in lists_at]
        hot = jnp.concatenate([h for h, _ in hots], axis=1)
        hi = jnp.concatenate([h for _, h in hots], axis=1)
        got = jnp.zeros((CW, len(hots) * HP), jnp.float32)
        step = 8
        for g in range(0, GP, step):
            part = jnp.dot(
                own[g : g + step].reshape(step * CW, LO), hot, preferred_element_type=jnp.float32
            )
            for h in range(step):
                got = jnp.where(hi == g + h, part[h * CW : (h + 1) * CW], got)
        got = got.astype(jnp.bfloat16)
        return [got[:, i * HP : (i + 1) * HP] for i in range(len(hots))]

    def node_copy(k, to, source):
        return pltpu.make_async_remote_copy(
            src_ref=packed.at[k],
            dst_ref=halo.at[source],
            send_sem=nsend.at[k],
            recv_sem=nrecv.at[k],
            device_id={"node": to},
            device_id_type=MESH,
        )

    def send_nodes(i, c):
        ks = [far_first(i) * XS + j for j in range(XS)]
        tos = [node_at(n, k) for k in ks]
        for k, to, got in zip(ks, tos, pick(tos)):
            packed[k] = got
            node_copy(k, to, n).start()
        return c

    lax.fori_loop(0, ZS - 1, send_nodes, 0)
    tos = [node_at(n, k) for k in range(XS)]
    for k, (to, got) in enumerate(zip(tos, pick(tos))):
        if k == 0:
            halo[n] = got
        else:
            packed[k] = got
            node_copy(k, to, n).start()

    def finish_node(i, c):
        k = NN - i
        node_copy(k, node_at(n, k), node_back(n, k)).wait()
        return c

    lax.fori_loop(1, NN, finish_node, 0)

    def finish_feat(k, c):
        feat_copy(k, feat_at(f, k), f).wait_send()
        return c

    lax.fori_loop(1, NF, finish_feat, 0)
    for k in (1, 3):
        rows_copy(k, (y + NY - k) & (NY - 1)).wait()
    for load in loads[3:]:
        load.wait()


def forward(features, weight, lists, adjacency, cotangent, coords):
    part = jax.ShapeDtypeStruct((GP, CW, LO), jnp.bfloat16)

    def like(a):
        return jax.ShapeDtypeStruct(a.shape, a.dtype)

    return pl.pallas_call(
        forward_kernel,
        out_shape=(
            part,
            part,
            jax.ShapeDtypeStruct((NY, RD, F), jnp.bfloat16),
            like(adjacency),
            like(cotangent),
            like(coords),
        ),
        in_specs=[pl.BlockSpec(memory_space=pltpu.HBM)] * 6,
        out_specs=(pl.BlockSpec(memory_space=VMEM),) * 6,
        scratch_shapes=[
            VMEM((F, F), jnp.bfloat16),
            VMEM((NN, HP), jnp.int32),
            VMEM((GD, F, LO), jnp.bfloat16),
            VMEM((NN, CW, HP), jnp.bfloat16),
            pltpu.SemaphoreType.DMA((NF,)),
            pltpu.SemaphoreType.DMA((NF,)),
            pltpu.SemaphoreType.DMA((NN,)),
            pltpu.SemaphoreType.DMA((NN,)),
            pltpu.SemaphoreType.DMA((NY,)),
            pltpu.SemaphoreType.DMA((NY,)),
            pltpu.SemaphoreType.DMA((6,)),
        ],
        compiler_params=pltpu.CompilerParams(
            collective_id=0, has_side_effects=True, vmem_limit_bytes=12 * 2**20
        ),
        name="project_and_send",
    )(
        *(
            pltpu.with_memory_space_constraint(a, pltpu.HBM)
            for a in (features, weight, lists, adjacency, cotangent, coords)
        )
    )


UNROLL = 64


def blocks_kernel(
    coords_v, counts, held, own, halo, cot, act, local, remote, coords, ext, pre, gpre, grad, sem
):
    load = pltpu.make_async_copy(coords_v, coords, sem)
    load.start()
    count = counts[0]
    pre[...] = jnp.zeros_like(pre)
    grad[...] = jnp.zeros_like(grad)
    for g in range(GP):
        for s in range(2):
            ext[2 * g + s] = own[g, :, s * BLK : (s + 1) * BLK]
            ext[ROWB + 2 * g + s] = halo[g, :, s * BLK : (s + 1) * BLK]
    load.wait()

    def row_of(b):
        return jnp.where(b < count, coords[0, b], ROWB)

    def gather(j, c):
        base = j * UNROLL
        terms = []
        for b in [base + u for u in range(0, UNROLL, 2)]:
            cols = jnp.concatenate([ext[coords[1, b]], ext[coords[1, b + 1]]], axis=0)
            pair = lax.dot_general(
                cols,
                held[pl.ds(b, 2)].reshape(2 * BLK, BLK),
                NT,
                preferred_element_type=jnp.float32,
            )
            terms += [pair[:CW, :BLK], pair[CW:, BLK:]]
        for u in range(UNROLL):
            r = row_of(base + u)
            pre[r] = pre[r] + terms[u]
        return c

    lax.fori_loop(0, MAXB // UNROLL, gather, 0)

    for r in range(ROWB):
        v = pre[r]
        at = slice(r * BLK, (r + 1) * BLK)
        sigma = jax.nn.sigmoid(v)
        act[:, at] = (v * sigma).astype(jnp.bfloat16)
        gpre[r] = (cot[:, at].astype(jnp.float32) * sigma * (1.0 + v * (1.0 - sigma))).astype(
            jnp.bfloat16
        )
    gpre[ROWB] = jnp.zeros((CW, BLK), jnp.bfloat16)

    def spread(j, c):
        base = j * UNROLL
        terms = []
        for b in [base + u for u in range(0, UNROLL, 2)]:
            rows = jnp.concatenate([gpre[row_of(b)], gpre[row_of(b + 1)]], axis=0)
            pair = jnp.dot(
                rows,
                jnp.concatenate([held[b], held[b + 1]], axis=1),
                preferred_element_type=jnp.float32,
            )
            terms += [pair[:CW, :BLK], pair[CW:, BLK:]]
        for u in range(UNROLL):
            col = coords[1, base + u]
            grad[col] = grad[col] + terms[u]
        return c

    lax.fori_loop(0, MAXB // UNROLL, spread, 0)
    for g in range(GP):
        for s in range(2):
            at = slice(s * BLK, (s + 1) * BLK)
            local[g, :, at] = grad[2 * g + s]
            remote[g, :, at] = grad[ROWB + 2 * g + s].astype(jnp.bfloat16)


def blocks(coords, counts, adjacency, own, halo, cotangent):
    return pl.pallas_call(
        blocks_kernel,
        out_shape=(
            jax.ShapeDtypeStruct((CW, ROWB * BLK), jnp.bfloat16),
            jax.ShapeDtypeStruct((GP, CW, LO), jnp.float32),
            jax.ShapeDtypeStruct((NN, CW, HP), jnp.bfloat16),
        ),
        in_specs=[
            pl.BlockSpec(memory_space=VMEM),
            pl.BlockSpec(memory_space=pltpu.SMEM),
            pl.BlockSpec(memory_space=VMEM),
            pl.BlockSpec(memory_space=VMEM),
            pl.BlockSpec(memory_space=VMEM),
            pl.BlockSpec(memory_space=VMEM),
        ],
        out_specs=(pl.BlockSpec(memory_space=VMEM),) * 3,
        scratch_shapes=[
            pltpu.SMEM((2, MAXB), jnp.int32),
            VMEM((COLB, CW, BLK), jnp.bfloat16),
            VMEM((ROWB + 1, CW, BLK), jnp.float32),
            VMEM((ROWB + 1, CW, BLK), jnp.bfloat16),
            VMEM((COLB, CW, BLK), jnp.float32),
            pltpu.SemaphoreType.DMA,
        ],
        compiler_params=pltpu.CompilerParams(vmem_limit_bytes=14 * 2**20),
        name="blocks",
    )(coords, counts, adjacency, own, halo, cotangent)


def backward_kernel(
    remote, local, lists, xs, w_ref, in_grad, w_grad,
    x_far, x_other, landed, acc, gz, gz_rows, pieces, pland, zpart, zland, whole,
    nsend, nrecv, fsend, frecv, xsend, xrecv, osend, orecv, psend, precv, zsend, zrecv, asend, arecv,
):
    n = lax.axis_index("node")
    f = lax.axis_index("feat")
    y = lax.shift_right_logical(f, 1)
    core = f & 1
    far = y ^ 2
    barrier = enter(n, f)
    acc[...] = local[...]

    def add(lists_at, vals):
        hots = [one_hot_t(lists, p) for p in lists_at]
        hot = jnp.concatenate([h for h, _ in hots], axis=1)
        step = 8
        for g in range(0, GP, step):
            rows = jnp.concatenate(
                [
                    jnp.concatenate(
                        [jnp.where(hi == g + h, v, 0.0).astype(jnp.bfloat16) for h in range(step)],
                        axis=0,
                    )
                    for (_, hi), v in zip(hots, vals)
                ],
                axis=1,
            )
            term = lax.dot_general(rows, hot, NT, preferred_element_type=jnp.float32)
            acc[g : g + step] = acc[g : g + step] + term.reshape(step, CW, LO)

    pl.semaphore_wait(barrier, NN + NF - 2)

    def node_copy(k, to, source):
        return pltpu.make_async_remote_copy(
            src_ref=remote.at[to],
            dst_ref=landed.at[source],
            send_sem=nsend.at[k],
            recv_sem=nrecv.at[k],
            device_id={"node": to},
            device_id_type=MESH,
        )

    for k in range(1, XS):
        node_copy(k, node_at(n, k), n).start()

    def start_nodes(i, c):
        for j in range(XS):
            k = far_first(i) * XS + j
            node_copy(k, node_at(n, k), n).start()
        return c

    lax.fori_loop(0, ZS - 1, start_nodes, 0)
    far_copy = pltpu.make_async_remote_copy(
        src_ref=xs.at[y],
        dst_ref=x_far,
        send_sem=xsend,
        recv_sem=xrecv,
        device_id={"feat": f ^ 4},
        device_id_type=MESH,
    )

    def other_copy(k, src):
        return pltpu.make_async_remote_copy(
            src_ref=src,
            dst_ref=x_other.at[(y + k) & (NY - 1)],
            send_sem=osend.at[k],
            recv_sem=orecv.at[k],
            device_id={"feat": f ^ 1},
            device_id_type=MESH,
        )

    far_copy.start()
    for k in (0, 1, 3):
        other_copy(k, xs.at[(y + k) & (NY - 1)]).start()
    sources = [node_back(n, k) for k in range(XS)]
    for k in range(1, XS):
        node_copy(k, node_at(n, k), sources[k]).wait_recv()
    landed[n] = remote[n]
    add(sources, [landed[p].astype(jnp.float32) for p in sources])

    def take_nodes(i, c):
        ks = [far_first(i) * XS + j for j in range(XS)]
        sources = [node_back(n, k) for k in ks]
        for k, p in zip(ks, sources):
            node_copy(k, node_at(n, k), p).wait_recv()
        add(sources, [landed[p].astype(jnp.float32) for p in sources])
        return c

    lax.fori_loop(0, ZS - 2, take_nodes, 0)
    far_copy.wait_recv()
    other_copy(2, x_far).start()
    take_nodes(ZS - 2, 0)
    gz[...] = acc[...].astype(jnp.bfloat16)

    def feat_copy(k, to, source):
        return pltpu.make_async_remote_copy(
            src_ref=gz.at[pl.ds(to * GD, GD)],
            dst_ref=gz_rows.at[:, pl.ds(pl.multiple_of(source * CW, CW), CW), :],
            send_sem=fsend.at[k],
            recv_sem=frecv.at[k],
            device_id={"feat": to},
            device_id_type=MESH,
        )

    def start_feat(k, c):
        feat_copy(k, feat_at(f, k), f).start()
        return c

    lax.fori_loop(1, NF, start_feat, 0)
    for k in range(NY):
        other_copy(k, x_far).wait_recv()

    def product(rows, at, group):
        out = jnp.zeros((CW, F), jnp.float32)
        for j in range(GD):
            out = out + jnp.dot(
                gz[group + j],
                rows[at, j * LO : (j + 1) * LO, :],
                preferred_element_type=jnp.float32,
            )
        return out

    mine = product(x_far.reshape(1, RD, F), 0, GD * (2 * far + core))
    for k in (0, 1, 3):
        at = (y + k) & (NY - 1)
        mine = mine + product(xs, at, GD * (2 * at + core))
    for at in range(NY):
        mine = mine + product(x_other, at, GD * (2 * at + 1 - core))
    mine = mine * (1.0 / math.sqrt(NN * ROWB * BLK))
    z, x = n & -XS, n & (XS - 1)
    pieces[...] = mine.reshape(XS, CW // XS, F)

    def x_at(k):
        return z + ((x + k) & (XS - 1))

    def z_at(k):
        return ((z + XS * k) & (NN - 1)) + x

    def share_copy(k, source):
        to = x_at(k)
        return pltpu.make_async_remote_copy(
            src_ref=pieces.at[to & (XS - 1)],
            dst_ref=pland.at[source & (XS - 1)],
            send_sem=psend.at[k],
            recv_sem=precv.at[k],
            device_id={"node": to},
            device_id_type=MESH,
        )

    for k in range(1, XS):
        share_copy(k, n).start()
    pland[x] = pieces[x]
    for k in range(1, XS):
        share_copy(k, x_at(XS - k)).wait_recv()
    zpart[...] = pland[0] + pland[1] + pland[2] + pland[3]

    def z_copy(k, source):
        return pltpu.make_async_remote_copy(
            src_ref=zpart,
            dst_ref=zland.at[lax.shift_right_logical(source, 2)],
            send_sem=zsend.at[k],
            recv_sem=zrecv.at[k],
            device_id={"node": z_at(k)},
            device_id_type=MESH,
        )

    for k in range(1, ZS):
        z_copy(k, n).start()

    gz_rows[:, pl.ds(pl.multiple_of(f * CW, CW), CW), :] = gz[pl.ds(f * GD, GD)]
    wt = w_ref[...].astype(jnp.float32).T.astype(jnp.bfloat16)

    def wait_feat(k, c):
        feat_copy(k, feat_at(f, k), feat_back(f, k)).wait_recv()
        return c

    lax.fori_loop(1, NF, wait_feat, 0)
    for h in range(GD):
        rows = gz_rows[h].astype(jnp.float32).T.astype(jnp.bfloat16)
        in_grad[h * LO : (h + 1) * LO, :] = jnp.dot(
            rows, wt, preferred_element_type=jnp.float32
        ).astype(jnp.bfloat16)

    zland[lax.shift_right_logical(n, 2)] = zpart[...]
    for k in range(1, ZS):
        z_copy(k, z_at(ZS - k)).wait_recv()
    summed = zland[0]
    for i in range(1, ZS):
        summed = summed + zland[i]
    whole[x] = summed

    def back_copy(k, source):
        return pltpu.make_async_remote_copy(
            src_ref=whole.at[x],
            dst_ref=whole.at[source & (XS - 1)],
            send_sem=asend.at[k],
            recv_sem=arecv.at[k],
            device_id={"node": x_at(k)},
            device_id_type=MESH,
        )

    for k in range(1, XS):
        back_copy(k, n).start()
    for k in range(1, XS):
        back_copy(k, x_at(XS - k)).wait_recv()
    w_grad[...] = whole[...].reshape(CW, F)
    for k in range(1, XS):
        share_copy(k, n).wait_send()
        back_copy(k, n).wait_send()
    for k in range(1, ZS):
        z_copy(k, n).wait_send()

    def finish_node(k, c):
        node_copy(k, node_at(n, k), n).wait_send()
        return c

    lax.fori_loop(1, NN, finish_node, 0)

    def finish_feat(k, c):
        feat_copy(k, feat_at(f, k), f).wait_send()
        return c

    lax.fori_loop(1, NF, finish_feat, 0)
    far_copy.wait_send()
    for k in range(NY):
        other_copy(k, x_far).wait_send()


def backward(remote, local, lists, xs, weight):
    dma = pltpu.SemaphoreType.DMA
    return pl.pallas_call(
        backward_kernel,
        out_shape=(
            jax.ShapeDtypeStruct((RD, F), jnp.bfloat16),
            jax.ShapeDtypeStruct((CW, F), jnp.float32),
        ),
        in_specs=[
            pl.BlockSpec(memory_space=VMEM),
            pl.BlockSpec(memory_space=VMEM),
            pl.BlockSpec(memory_space=VMEM),
            pl.BlockSpec(memory_space=VMEM),
            pl.BlockSpec(memory_space=VMEM),
        ],
        out_specs=(pl.BlockSpec(memory_space=VMEM),) * 2,
        scratch_shapes=[
            VMEM((RD, F), jnp.bfloat16),
            VMEM((NY, RD, F), jnp.bfloat16),
            VMEM((NN, CW, HP), jnp.bfloat16),
            VMEM((GP, CW, LO), jnp.float32),
            VMEM((GP, CW, LO), jnp.bfloat16),
            VMEM((GD, F, LO), jnp.bfloat16),
            VMEM((XS, CW // XS, F), jnp.float32),
            VMEM((XS, CW // XS, F), jnp.float32),
            VMEM((CW // XS, F), jnp.float32),
            VMEM((ZS, CW // XS, F), jnp.float32),
            VMEM((XS, CW // XS, F), jnp.float32),
            dma((NN,)),
            dma((NN,)),
            dma((NF,)),
            dma((NF,)),
            dma,
            dma,
            dma((NY,)),
            dma((NY,)),
            dma((XS,)),
            dma((XS,)),
            dma((ZS,)),
            dma((ZS,)),
            dma((XS,)),
            dma((XS,)),
        ],
        compiler_params=pltpu.CompilerParams(
            collective_id=1, has_side_effects=True, vmem_limit_bytes=32 * 2**20
        ),
        name="return_and_sum",
    )(remote, local, lists, xs, weight)


def body(features, weight, adjacency, block_coords, block_counts, send_rows, cotangent):
    own, halo, xs, held, cot, coords = forward(
        features, weight, send_rows, adjacency, cotangent, block_coords
    )
    activations, local, remote = blocks(coords, block_counts, held, own, halo, cot)
    input_grad, weight_grad_t = backward(remote, local, send_rows, xs, weight)
    weight_grad = weight_grad_t.T
    return (activations, input_grad, weight_grad)


def solution(mesh):
    return jax.shard_map(
        body,
        mesh=mesh,
        in_specs=(
            P(("node", "feat"), None),
            P(),
            P("node", None, None),
            P(None, "node"),
            P("node"),
            P("node", None),
            P("feat", "node"),
        ),
        out_specs=(P("feat", "node"), P(("node", "feat"), None), P(None, "feat")),
        check_vma=False,
    )
```

```python
import functools
import math

import jax
import jax.numpy as jnp
from jax import lax
from jax.experimental import pallas as pl
from jax.experimental.pallas import tpu as pltpu
from jax.sharding import PartitionSpec as P

ZS, XS = 8, 4
NN = ZS * XS
NF = 8
NY = 4
F = 256
CW = F // NF
RD = 1024
LO = 256
GD = RD // LO
GP = NF * GD
HP = 256
BLK = 128
NT = (((1,), (1,)), ((), ()))
ROWB = 64
COLB = 128
MAXB = 512
MESH = pl.DeviceIdType.MESH
VMEM = pltpu.VMEM


def node_at(n, k):
    z = ((n & -XS) + (k & -XS)) & (NN - 1)
    x = (n + k) & (XS - 1)
    return z + x


def node_back(n, k):
    z = ((n & -XS) + NN - (k & -XS)) & (NN - 1)
    x = (n + XS - (k & (XS - 1))) & (XS - 1)
    return z + x


def far_first(i):
    return ZS // 2 + (i // 2) * (1 - (i & 1)) - ((i + 1) // 2) * (i & 1)


def feat_at(f, k):
    return (f + k) & (NF - 1)


def feat_back(f, k):
    return (f + NF - k) & (NF - 1)


def enter(n, f):
    barrier = pltpu.get_barrier_semaphore()

    def greet_node(k, c):
        pl.semaphore_signal(barrier, inc=1, device_id={"node": node_at(n, k)}, device_id_type=MESH)
        return c

    def greet_feat(k, c):
        pl.semaphore_signal(barrier, inc=1, device_id={"feat": feat_at(f, k)}, device_id_type=MESH)
        return c

    lax.fori_loop(1, NF, greet_feat, 0)
    lax.fori_loop(1, NN, greet_node, 0)
    return barrier


def one_hot_t(lists, p):
    idx = lists[pl.ds(p, 1), :]
    lo = idx & (LO - 1)
    hi = lax.shift_right_logical(idx, 8)
    rows = lax.broadcasted_iota(jnp.int32, (LO, HP), 0)
    return (rows == lo).astype(jnp.float32).astype(jnp.bfloat16), hi


def forward_kernel(
    x_hbm, w_hbm, lists_hbm, adj_hbm, cot_hbm, coords_hbm,
    own, halo, xs, adj, cot, coords,
    w_ref, lists, proj, packed, fsend, frecv, nsend, nrecv, xsend, xrecv, lsem,
):
    n = lax.axis_index("node")
    f = lax.axis_index("feat")
    y = lax.shift_right_logical(f, 1)
    x_ref = xs.at[y]
    loads = [
        pltpu.make_async_copy(src, dst, lsem.at[i])
        for i, (src, dst) in enumerate(
            [
                (x_hbm, x_ref),
                (w_hbm, w_ref),
                (lists_hbm, lists),
                (coords_hbm, coords),
                (cot_hbm, cot),
                (adj_hbm, adj),
            ]
        )
    ]
    for load in loads:
        load.start()
    barrier = enter(n, f)
    loads[0].wait()
    loads[1].wait()
    wt = w_ref[...].astype(jnp.float32).T.astype(jnp.bfloat16)
    for h in range(GD):
        proj[h] = lax.dot_general(
            wt,
            xs[y, h * LO : (h + 1) * LO, :],
            (((1,), (1,)), ((), ())),
            preferred_element_type=jnp.float32,
        ).astype(jnp.bfloat16)
    pl.semaphore_wait(barrier, NN + NF - 2)

    def feat_copy(k, to, source):
        return pltpu.make_async_remote_copy(
            src_ref=proj.at[:, pl.ds(pl.multiple_of(to * CW, CW), CW), :],
            dst_ref=own.at[pl.ds(source * GD, GD)],
            send_sem=fsend.at[k],
            recv_sem=frecv.at[k],
            device_id={"feat": to},
            device_id_type=MESH,
        )

    def start_feat(k, c):
        feat_copy(k, feat_at(f, k), f).start()
        return c

    lax.fori_loop(1, NF, start_feat, 0)
    loads[2].wait()
    own[pl.ds(f * GD, GD)] = proj[:, pl.ds(pl.multiple_of(f * CW, CW), CW), :]

    def wait_feat(k, c):
        feat_copy(k, feat_at(f, k), feat_back(f, k)).wait_recv()
        return c

    lax.fori_loop(1, NF, wait_feat, 0)

    def rows_copy(k, source):
        return pltpu.make_async_remote_copy(
            src_ref=xs.at[y],
            dst_ref=xs.at[source],
            send_sem=xsend.at[k],
            recv_sem=xrecv.at[k],
            device_id={"feat": feat_at(f, 2 * k)},
            device_id_type=MESH,
        )

    for k in (1, 3):
        rows_copy(k, y).start()

    def pick(lists_at):
        hots = [one_hot_t(lists, p) for p in lists_at]
        hot = jnp.concatenate([h for h, _ in hots], axis=1)
        hi = jnp.concatenate([h for _, h in hots], axis=1)
        got = jnp.zeros((CW, len(hots) * HP), jnp.float32)
        step = 8
        for g in range(0, GP, step):
            part = jnp.dot(
                own[g : g + step].reshape(step * CW, LO), hot, preferred_element_type=jnp.float32
            )
            for h in range(step):
                got = jnp.where(hi == g + h, part[h * CW : (h + 1) * CW], got)
        got = got.astype(jnp.bfloat16)
        return [got[:, i * HP : (i + 1) * HP] for i in range(len(hots))]

    def node_copy(k, to, source):
        return pltpu.make_async_remote_copy(
            src_ref=packed.at[k],
            dst_ref=halo.at[source],
            send_sem=nsend.at[k],
            recv_sem=nrecv.at[k],
            device_id={"node": to},
            device_id_type=MESH,
        )

    def send_nodes(i, c):
        ks = [far_first(i) * XS + j for j in range(XS)]
        tos = [node_at(n, k) for k in ks]
        for k, to, got in zip(ks, tos, pick(tos)):
            packed[k] = got
            node_copy(k, to, n).start()
        return c

    lax.fori_loop(0, ZS - 1, send_nodes, 0)
    tos = [node_at(n, k) for k in range(XS)]
    for k, (to, got) in enumerate(zip(tos, pick(tos))):
        if k == 0:
            halo[n] = got
        else:
            packed[k] = got
            node_copy(k, to, n).start()

    def finish_node(i, c):
        k = NN - i
        node_copy(k, node_at(n, k), node_back(n, k)).wait()
        return c

    lax.fori_loop(1, NN, finish_node, 0)

    def finish_feat(k, c):
        feat_copy(k, feat_at(f, k), f).wait_send()
        return c

    lax.fori_loop(1, NF, finish_feat, 0)
    for k in (1, 3):
        rows_copy(k, (y + NY - k) & (NY - 1)).wait()
    for load in loads[3:]:
        load.wait()


def forward(features, weight, lists, adjacency, cotangent, coords):
    part = jax.ShapeDtypeStruct((GP, CW, LO), jnp.bfloat16)

    def like(a):
        return jax.ShapeDtypeStruct(a.shape, a.dtype)

    return pl.pallas_call(
        forward_kernel,
        out_shape=(
            part,
            part,
            jax.ShapeDtypeStruct((NY, RD, F), jnp.bfloat16),
            like(adjacency),
            like(cotangent),
            like(coords),
        ),
        in_specs=[pl.BlockSpec(memory_space=pltpu.HBM)] * 6,
        out_specs=(pl.BlockSpec(memory_space=VMEM),) * 6,
        scratch_shapes=[
            VMEM((F, F), jnp.bfloat16),
            VMEM((NN, HP), jnp.int32),
            VMEM((GD, F, LO), jnp.bfloat16),
            VMEM((NN, CW, HP), jnp.bfloat16),
            pltpu.SemaphoreType.DMA((NF,)),
            pltpu.SemaphoreType.DMA((NF,)),
            pltpu.SemaphoreType.DMA((NN,)),
            pltpu.SemaphoreType.DMA((NN,)),
            pltpu.SemaphoreType.DMA((NY,)),
            pltpu.SemaphoreType.DMA((NY,)),
            pltpu.SemaphoreType.DMA((6,)),
        ],
        compiler_params=pltpu.CompilerParams(
            collective_id=0, has_side_effects=True, vmem_limit_bytes=12 * 2**20
        ),
        name="project_and_send",
    )(
        *(
            pltpu.with_memory_space_constraint(a, pltpu.HBM)
            for a in (features, weight, lists, adjacency, cotangent, coords)
        )
    )


UNROLL = 128
WIDE = 4


def blocks_kernel(
    coords_v, counts, held, own, halo, cot, act, local, remote, coords, ext, pre, gpre, grad, sem
):
    load = pltpu.make_async_copy(coords_v, coords, sem)
    load.start()
    count = counts[0]
    pre[...] = jnp.zeros_like(pre)
    grad[...] = jnp.zeros_like(grad)
    for g in range(GP):
        for s in range(2):
            ext[2 * g + s] = own[g, :, s * BLK : (s + 1) * BLK]
            ext[ROWB + 2 * g + s] = halo[g, :, s * BLK : (s + 1) * BLK]
    load.wait()

    def row_of(b):
        return jnp.where(b < count, coords[0, b], ROWB)

    def gather(j, c):
        base = j * UNROLL
        terms = []
        for b in [base + u for u in range(0, UNROLL, WIDE)]:
            cols = jnp.concatenate([ext[coords[1, b + i]] for i in range(WIDE)], axis=0)
            part = lax.dot_general(
                cols,
                held[pl.ds(b, WIDE)].reshape(WIDE * BLK, BLK),
                NT,
                preferred_element_type=jnp.float32,
            )
            for i in range(WIDE):
                terms.append(part[i * CW : (i + 1) * CW, i * BLK : (i + 1) * BLK])
        for u in range(UNROLL):
            r = row_of(base + u)
            pre[r] = pre[r] + terms[u]
        return c

    lax.fori_loop(0, MAXB // UNROLL, gather, 0)

    for r in range(ROWB):
        v = pre[r]
        at = slice(r * BLK, (r + 1) * BLK)
        sigma = jax.nn.sigmoid(v)
        act[:, at] = (v * sigma).astype(jnp.bfloat16)
        gpre[r] = (cot[:, at].astype(jnp.float32) * sigma * (1.0 + v * (1.0 - sigma))).astype(
            jnp.bfloat16
        )
    gpre[ROWB] = jnp.zeros((CW, BLK), jnp.bfloat16)

    def spread(j, c):
        base = j * UNROLL
        terms = []
        for b in [base + u for u in range(0, UNROLL, 2)]:
            rows = jnp.concatenate([gpre[row_of(b)], gpre[row_of(b + 1)]], axis=0)
            pair = jnp.dot(
                rows,
                jnp.concatenate([held[b], held[b + 1]], axis=1),
                preferred_element_type=jnp.float32,
            )
            terms += [pair[:CW, :BLK], pair[CW:, BLK:]]
        for u in range(UNROLL):
            col = coords[1, base + u]
            grad[col] = grad[col] + terms[u]
        return c

    lax.fori_loop(0, MAXB // UNROLL, spread, 0)
    for g in range(GP):
        for s in range(2):
            at = slice(s * BLK, (s + 1) * BLK)
            local[g, :, at] = grad[2 * g + s]
            remote[g, :, at] = grad[ROWB + 2 * g + s].astype(jnp.bfloat16)


def blocks(coords, counts, adjacency, own, halo, cotangent):
    return pl.pallas_call(
        blocks_kernel,
        out_shape=(
            jax.ShapeDtypeStruct((CW, ROWB * BLK), jnp.bfloat16),
            jax.ShapeDtypeStruct((GP, CW, LO), jnp.float32),
            jax.ShapeDtypeStruct((NN, CW, HP), jnp.bfloat16),
        ),
        in_specs=[
            pl.BlockSpec(memory_space=VMEM),
            pl.BlockSpec(memory_space=pltpu.SMEM),
            pl.BlockSpec(memory_space=VMEM),
            pl.BlockSpec(memory_space=VMEM),
            pl.BlockSpec(memory_space=VMEM),
            pl.BlockSpec(memory_space=VMEM),
        ],
        out_specs=(pl.BlockSpec(memory_space=VMEM),) * 3,
        scratch_shapes=[
            pltpu.SMEM((2, MAXB), jnp.int32),
            VMEM((COLB, CW, BLK), jnp.bfloat16),
            VMEM((ROWB + 1, CW, BLK), jnp.float32),
            VMEM((ROWB + 1, CW, BLK), jnp.bfloat16),
            VMEM((COLB, CW, BLK), jnp.float32),
            pltpu.SemaphoreType.DMA,
        ],
        compiler_params=pltpu.CompilerParams(vmem_limit_bytes=14 * 2**20),
        name="blocks",
    )(coords, counts, adjacency, own, halo, cotangent)


def backward_kernel(
    remote, local, lists, xs, w_ref, in_grad, w_grad,
    x_far, x_other, landed, acc, gz, gz_rows, pieces, pland, zpart, zland, whole,
    nsend, nrecv, fsend, frecv, xsend, xrecv, osend, orecv, psend, precv, zsend, zrecv, asend, arecv,
):
    n = lax.axis_index("node")
    f = lax.axis_index("feat")
    y = lax.shift_right_logical(f, 1)
    core = f & 1
    far = y ^ 2
    barrier = enter(n, f)

    def add(lists_at, vals):
        hots = [one_hot_t(lists, p) for p in lists_at]
        hot = jnp.concatenate([h for h, _ in hots], axis=1)
        step = 8
        for g in range(0, GP, step):
            rows = jnp.concatenate(
                [
                    jnp.concatenate(
                        [jnp.where(hi == g + h, v, 0.0).astype(jnp.bfloat16) for h in range(step)],
                        axis=0,
                    )
                    for (_, hi), v in zip(hots, vals)
                ],
                axis=1,
            )
            term = lax.dot_general(rows, hot, NT, preferred_element_type=jnp.float32)
            acc[g : g + step] = acc[g : g + step] + term.reshape(step, CW, LO)

    pl.semaphore_wait(barrier, NN + NF - 2)

    def node_copy(k, to, source):
        return pltpu.make_async_remote_copy(
            src_ref=remote.at[to],
            dst_ref=landed.at[source],
            send_sem=nsend.at[k],
            recv_sem=nrecv.at[k],
            device_id={"node": to},
            device_id_type=MESH,
        )

    for k in range(1, XS):
        node_copy(k, node_at(n, k), n).start()

    def start_nodes(i, c):
        for j in range(XS):
            k = far_first(i) * XS + j
            node_copy(k, node_at(n, k), n).start()
        return c

    lax.fori_loop(0, ZS - 1, start_nodes, 0)
    far_copy = pltpu.make_async_remote_copy(
        src_ref=xs.at[y],
        dst_ref=x_far,
        send_sem=xsend,
        recv_sem=xrecv,
        device_id={"feat": f ^ 4},
        device_id_type=MESH,
    )

    def other_copy(k, src):
        return pltpu.make_async_remote_copy(
            src_ref=src,
            dst_ref=x_other.at[(y + k) & (NY - 1)],
            send_sem=osend.at[k],
            recv_sem=orecv.at[k],
            device_id={"feat": f ^ 1},
            device_id_type=MESH,
        )

    far_copy.start()
    for k in (0, 1, 3):
        other_copy(k, xs.at[(y + k) & (NY - 1)]).start()
    acc[...] = local[...]
    sources = [node_back(n, k) for k in range(XS)]
    for k in range(1, XS):
        node_copy(k, node_at(n, k), sources[k]).wait_recv()
    landed[n] = remote[n]
    add(sources, [landed[p].astype(jnp.float32) for p in sources])

    def take_nodes(i, c):
        ks = [far_first(i) * XS + j for j in range(XS)]
        sources = [node_back(n, k) for k in ks]
        for k, p in zip(ks, sources):
            node_copy(k, node_at(n, k), p).wait_recv()
        add(sources, [landed[p].astype(jnp.float32) for p in sources])
        return c

    lax.fori_loop(0, ZS - 2, take_nodes, 0)
    far_copy.wait_recv()
    other_copy(2, x_far).start()
    take_nodes(ZS - 2, 0)
    gz[...] = acc[...].astype(jnp.bfloat16)

    def feat_copy(k, to, source):
        return pltpu.make_async_remote_copy(
            src_ref=gz.at[pl.ds(to * GD, GD)],
            dst_ref=gz_rows.at[:, pl.ds(pl.multiple_of(source * CW, CW), CW), :],
            send_sem=fsend.at[k],
            recv_sem=frecv.at[k],
            device_id={"feat": to},
            device_id_type=MESH,
        )

    def start_feat(k, c):
        feat_copy(k, feat_at(f, k), f).start()
        return c

    lax.fori_loop(1, NF, start_feat, 0)
    for k in range(NY):
        other_copy(k, x_far).wait_recv()

    def product(rows, at, group):
        out = jnp.zeros((CW, F), jnp.float32)
        for j in range(GD):
            out = out + jnp.dot(
                gz[group + j],
                rows[at, j * LO : (j + 1) * LO, :],
                preferred_element_type=jnp.float32,
            )
        return out

    mine = product(x_far.reshape(1, RD, F), 0, GD * (2 * far + core))
    for k in (0, 1, 3):
        at = (y + k) & (NY - 1)
        mine = mine + product(xs, at, GD * (2 * at + core))
    for at in range(NY):
        mine = mine + product(x_other, at, GD * (2 * at + 1 - core))
    mine = mine * (1.0 / math.sqrt(NN * ROWB * BLK))
    z, x = n & -XS, n & (XS - 1)
    pieces[...] = mine.reshape(XS, CW // XS, F)

    def x_at(k):
        return z + ((x + k) & (XS - 1))

    def z_at(k):
        return ((z + XS * k) & (NN - 1)) + x

    def share_copy(k, source):
        to = x_at(k)
        return pltpu.make_async_remote_copy(
            src_ref=pieces.at[to & (XS - 1)],
            dst_ref=pland.at[source & (XS - 1)],
            send_sem=psend.at[k],
            recv_sem=precv.at[k],
            device_id={"node": to},
            device_id_type=MESH,
        )

    for k in range(1, XS):
        share_copy(k, n).start()
    pland[x] = pieces[x]
    for k in range(1, XS):
        share_copy(k, x_at(XS - k)).wait_recv()
    zpart[...] = pland[0] + pland[1] + pland[2] + pland[3]

    def z_copy(k, source):
        return pltpu.make_async_remote_copy(
            src_ref=zpart,
            dst_ref=zland.at[lax.shift_right_logical(source, 2)],
            send_sem=zsend.at[k],
            recv_sem=zrecv.at[k],
            device_id={"node": z_at(k)},
            device_id_type=MESH,
        )

    for k in range(1, ZS):
        z_copy(k, n).start()

    gz_rows[:, pl.ds(pl.multiple_of(f * CW, CW), CW), :] = gz[pl.ds(f * GD, GD)]
    wt = w_ref[...].astype(jnp.float32).T.astype(jnp.bfloat16)

    def wait_feat(k, c):
        feat_copy(k, feat_at(f, k), feat_back(f, k)).wait_recv()
        return c

    lax.fori_loop(1, NF, wait_feat, 0)
    for h in range(GD):
        rows = gz_rows[h].astype(jnp.float32).T.astype(jnp.bfloat16)
        in_grad[h * LO : (h + 1) * LO, :] = jnp.dot(
            rows, wt, preferred_element_type=jnp.float32
        ).astype(jnp.bfloat16)

    zland[lax.shift_right_logical(n, 2)] = zpart[...]
    for k in range(1, ZS):
        z_copy(k, z_at(ZS - k)).wait_recv()
    summed = zland[0]
    for i in range(1, ZS):
        summed = summed + zland[i]
    whole[x] = summed

    def back_copy(k, source):
        return pltpu.make_async_remote_copy(
            src_ref=whole.at[x],
            dst_ref=whole.at[source & (XS - 1)],
            send_sem=asend.at[k],
            recv_sem=arecv.at[k],
            device_id={"node": x_at(k)},
            device_id_type=MESH,
        )

    for k in range(1, XS):
        back_copy(k, n).start()
    for k in range(1, XS):
        back_copy(k, x_at(XS - k)).wait_recv()
    w_grad[...] = whole[...].reshape(CW, F)
    for k in range(1, XS):
        share_copy(k, n).wait_send()
        back_copy(k, n).wait_send()
    for k in range(1, ZS):
        z_copy(k, n).wait_send()

    def finish_node(k, c):
        node_copy(k, node_at(n, k), n).wait_send()
        return c

    lax.fori_loop(1, NN, finish_node, 0)

    def finish_feat(k, c):
        feat_copy(k, feat_at(f, k), f).wait_send()
        return c

    lax.fori_loop(1, NF, finish_feat, 0)
    far_copy.wait_send()
    for k in range(NY):
        other_copy(k, x_far).wait_send()


def backward(remote, local, lists, xs, weight):
    dma = pltpu.SemaphoreType.DMA
    return pl.pallas_call(
        backward_kernel,
        out_shape=(
            jax.ShapeDtypeStruct((RD, F), jnp.bfloat16),
            jax.ShapeDtypeStruct((CW, F), jnp.float32),
        ),
        in_specs=[
            pl.BlockSpec(memory_space=VMEM),
            pl.BlockSpec(memory_space=VMEM),
            pl.BlockSpec(memory_space=VMEM),
            pl.BlockSpec(memory_space=VMEM),
            pl.BlockSpec(memory_space=VMEM),
        ],
        out_specs=(pl.BlockSpec(memory_space=VMEM),) * 2,
        scratch_shapes=[
            VMEM((RD, F), jnp.bfloat16),
            VMEM((NY, RD, F), jnp.bfloat16),
            VMEM((NN, CW, HP), jnp.bfloat16),
            VMEM((GP, CW, LO), jnp.float32),
            VMEM((GP, CW, LO), jnp.bfloat16),
            VMEM((GD, F, LO), jnp.bfloat16),
            VMEM((XS, CW // XS, F), jnp.float32),
            VMEM((XS, CW // XS, F), jnp.float32),
            VMEM((CW // XS, F), jnp.float32),
            VMEM((ZS, CW // XS, F), jnp.float32),
            VMEM((XS, CW // XS, F), jnp.float32),
            dma((NN,)),
            dma((NN,)),
            dma((NF,)),
            dma((NF,)),
            dma,
            dma,
            dma((NY,)),
            dma((NY,)),
            dma((XS,)),
            dma((XS,)),
            dma((ZS,)),
            dma((ZS,)),
            dma((XS,)),
            dma((XS,)),
        ],
        compiler_params=pltpu.CompilerParams(
            collective_id=1, has_side_effects=True, vmem_limit_bytes=32 * 2**20
        ),
        name="return_and_sum",
    )(remote, local, lists, xs, weight)


def body(features, weight, adjacency, block_coords, block_counts, send_rows, cotangent):
    own, halo, xs, held, cot, coords = forward(
        features, weight, send_rows, adjacency, cotangent, block_coords
    )
    activations, local, remote = blocks(coords, block_counts, held, own, halo, cot)
    input_grad, weight_grad_t = backward(remote, local, send_rows, xs, weight)
    weight_grad = weight_grad_t.T
    return (activations, input_grad, weight_grad)


def solution(mesh):
    return jax.shard_map(
        body,
        mesh=mesh,
        in_specs=(
            P(("node", "feat"), None),
            P(),
            P("node", None, None),
            P(None, "node"),
            P("node"),
            P("node", None),
            P("feat", "node"),
        ),
        out_specs=(P("feat", "node"), P(("node", "feat"), None), P(None, "feat")),
        check_vma=False,
    )
```

```python
import functools
import math

import jax
import jax.numpy as jnp
from jax import lax
from jax.experimental import pallas as pl
from jax.experimental.pallas import tpu as pltpu
from jax.sharding import PartitionSpec as P

ZS, XS = 8, 4
NN = ZS * XS
NF = 8
NY = 4
F = 256
CW = F // NF
RD = 1024
LO = 256
GD = RD // LO
GP = NF * GD
HP = 256
BLK = 128
NT = (((1,), (1,)), ((), ()))
ROWB = 64
COLB = 128
MAXB = 512
MESH = pl.DeviceIdType.MESH
VMEM = pltpu.VMEM


def node_at(n, k):
    z = ((n & -XS) + (k & -XS)) & (NN - 1)
    x = (n + k) & (XS - 1)
    return z + x


def node_back(n, k):
    z = ((n & -XS) + NN - (k & -XS)) & (NN - 1)
    x = (n + XS - (k & (XS - 1))) & (XS - 1)
    return z + x


def far_first(i):
    return ZS // 2 + (i // 2) * (1 - (i & 1)) - ((i + 1) // 2) * (i & 1)


def feat_at(f, k):
    return (f + k) & (NF - 1)


def feat_back(f, k):
    return (f + NF - k) & (NF - 1)


def enter(n, f):
    barrier = pltpu.get_barrier_semaphore()

    def greet_node(k, c):
        pl.semaphore_signal(barrier, inc=1, device_id={"node": node_at(n, k)}, device_id_type=MESH)
        return c

    def greet_feat(k, c):
        pl.semaphore_signal(barrier, inc=1, device_id={"feat": feat_at(f, k)}, device_id_type=MESH)
        return c

    lax.fori_loop(1, NF, greet_feat, 0)
    lax.fori_loop(1, NN, greet_node, 0)
    return barrier


def one_hot_t(lists, p):
    idx = lists[pl.ds(p, 1), :]
    lo = idx & (LO - 1)
    hi = lax.shift_right_logical(idx, 8)
    rows = lax.broadcasted_iota(jnp.int32, (LO, HP), 0)
    return (rows == lo).astype(jnp.float32).astype(jnp.bfloat16), hi


def forward_kernel(
    x_hbm, w_hbm, lists_hbm, adj_hbm, cot_hbm, coords_hbm,
    own, halo, xs, adj, cot, coords,
    w_ref, lists, proj, packed, fsend, frecv, nsend, nrecv, xsend, xrecv, lsem,
):
    n = lax.axis_index("node")
    f = lax.axis_index("feat")
    y = lax.shift_right_logical(f, 1)
    x_ref = xs.at[y]
    loads = [
        pltpu.make_async_copy(src, dst, lsem.at[i])
        for i, (src, dst) in enumerate(
            [
                (x_hbm, x_ref),
                (w_hbm, w_ref),
                (lists_hbm, lists),
                (coords_hbm, coords),
                (cot_hbm, cot),
                (adj_hbm, adj),
            ]
        )
    ]
    for load in loads:
        load.start()
    barrier = enter(n, f)
    loads[0].wait()
    loads[1].wait()
    wt = w_ref[...].astype(jnp.float32).T.astype(jnp.bfloat16)
    for h in range(GD):
        proj[h] = lax.dot_general(
            wt,
            xs[y, h * LO : (h + 1) * LO, :],
            (((1,), (1,)), ((), ())),
            preferred_element_type=jnp.float32,
        ).astype(jnp.bfloat16)
    pl.semaphore_wait(barrier, NN + NF - 2)

    def feat_copy(k, to, source):
        return pltpu.make_async_remote_copy(
            src_ref=proj.at[:, pl.ds(pl.multiple_of(to * CW, CW), CW), :],
            dst_ref=own.at[pl.ds(source * GD, GD)],
            send_sem=fsend.at[k],
            recv_sem=frecv.at[k],
            device_id={"feat": to},
            device_id_type=MESH,
        )

    def start_feat(k, c):
        feat_copy(k, feat_at(f, k), f).start()
        return c

    lax.fori_loop(1, NF, start_feat, 0)
    loads[2].wait()
    own[pl.ds(f * GD, GD)] = proj[:, pl.ds(pl.multiple_of(f * CW, CW), CW), :]

    def wait_feat(k, c):
        feat_copy(k, feat_at(f, k), feat_back(f, k)).wait_recv()
        return c

    lax.fori_loop(1, NF, wait_feat, 0)

    def rows_copy(k, source):
        return pltpu.make_async_remote_copy(
            src_ref=xs.at[y],
            dst_ref=xs.at[source],
            send_sem=xsend.at[k],
            recv_sem=xrecv.at[k],
            device_id={"feat": feat_at(f, 2 * k)},
            device_id_type=MESH,
        )

    for k in (1, 3):
        rows_copy(k, y).start()

    def pick(lists_at):
        hots = [one_hot_t(lists, p) for p in lists_at]
        hot = jnp.concatenate([h for h, _ in hots], axis=1)
        hi = jnp.concatenate([h for _, h in hots], axis=1)
        got = jnp.zeros((CW, len(hots) * HP), jnp.float32)
        step = 8
        for g in range(0, GP, step):
            part = jnp.dot(
                own[g : g + step].reshape(step * CW, LO), hot, preferred_element_type=jnp.float32
            )
            for h in range(step):
                got = jnp.where(hi == g + h, part[h * CW : (h + 1) * CW], got)
        got = got.astype(jnp.bfloat16)
        return [got[:, i * HP : (i + 1) * HP] for i in range(len(hots))]

    def node_copy(k, to, source):
        return pltpu.make_async_remote_copy(
            src_ref=packed.at[k],
            dst_ref=halo.at[source],
            send_sem=nsend.at[k],
            recv_sem=nrecv.at[k],
            device_id={"node": to},
            device_id_type=MESH,
        )

    def send_some(ks):
        tos = [node_at(n, k) for k in ks]
        for k, to, got in zip(ks, tos, pick(tos)):
            packed[k] = got
            node_copy(k, to, n).start()

    def send_nodes(i, c):
        send_some([far_first(i) * XS + j for j in range(XS)])
        return c

    first = far_first(0) * XS
    send_some([first])
    send_some([first + j for j in range(1, XS)])
    lax.fori_loop(1, ZS - 1, send_nodes, 0)
    tos = [node_at(n, k) for k in range(XS)]
    for k, (to, got) in enumerate(zip(tos, pick(tos))):
        if k == 0:
            halo[n] = got
        else:
            packed[k] = got
            node_copy(k, to, n).start()

    def finish_node(i, c):
        k = NN - i
        node_copy(k, node_at(n, k), node_back(n, k)).wait()
        return c

    lax.fori_loop(1, NN, finish_node, 0)

    def finish_feat(k, c):
        feat_copy(k, feat_at(f, k), f).wait_send()
        return c

    lax.fori_loop(1, NF, finish_feat, 0)
    for k in (1, 3):
        rows_copy(k, (y + NY - k) & (NY - 1)).wait()
    for load in loads[3:]:
        load.wait()


def forward(features, weight, lists, adjacency, cotangent, coords):
    part = jax.ShapeDtypeStruct((GP, CW, LO), jnp.bfloat16)

    def like(a):
        return jax.ShapeDtypeStruct(a.shape, a.dtype)

    return pl.pallas_call(
        forward_kernel,
        out_shape=(
            part,
            part,
            jax.ShapeDtypeStruct((NY, RD, F), jnp.bfloat16),
            like(adjacency),
            like(cotangent),
            like(coords),
        ),
        in_specs=[pl.BlockSpec(memory_space=pltpu.HBM)] * 6,
        out_specs=(pl.BlockSpec(memory_space=VMEM),) * 6,
        scratch_shapes=[
            VMEM((F, F), jnp.bfloat16),
            VMEM((NN, HP), jnp.int32),
            VMEM((GD, F, LO), jnp.bfloat16),
            VMEM((NN, CW, HP), jnp.bfloat16),
            pltpu.SemaphoreType.DMA((NF,)),
            pltpu.SemaphoreType.DMA((NF,)),
            pltpu.SemaphoreType.DMA((NN,)),
            pltpu.SemaphoreType.DMA((NN,)),
            pltpu.SemaphoreType.DMA((NY,)),
            pltpu.SemaphoreType.DMA((NY,)),
            pltpu.SemaphoreType.DMA((6,)),
        ],
        compiler_params=pltpu.CompilerParams(
            collective_id=0, has_side_effects=True, vmem_limit_bytes=12 * 2**20
        ),
        name="project_and_send",
    )(
        *(
            pltpu.with_memory_space_constraint(a, pltpu.HBM)
            for a in (features, weight, lists, adjacency, cotangent, coords)
        )
    )


UNROLL = 128
WIDE = 4


def blocks_kernel(
    coords_v, counts, held, own, halo, cot, act, local, remote, coords, ext, pre, gpre, grad, sem
):
    load = pltpu.make_async_copy(coords_v, coords, sem)
    load.start()
    count = counts[0]
    pre[ROWB] = jnp.zeros((CW, BLK), jnp.float32)
    for g in range(GP):
        for s in range(2):
            ext[2 * g + s] = own[g, :, s * BLK : (s + 1) * BLK]
            ext[ROWB + 2 * g + s] = halo[g, :, s * BLK : (s + 1) * BLK]
    load.wait()

    def row_of(b):
        return jnp.where(b < count, coords[0, b], ROWB)

    def gather(j, c, stored=0):
        base = j * UNROLL
        terms = []
        for b in [base + u for u in range(0, UNROLL, WIDE)]:
            cols = jnp.concatenate([ext[coords[1, b + i]] for i in range(WIDE)], axis=0)
            part = lax.dot_general(
                cols,
                held[pl.ds(b, WIDE)].reshape(WIDE * BLK, BLK),
                NT,
                preferred_element_type=jnp.float32,
            )
            for i in range(WIDE):
                terms.append(part[i * CW : (i + 1) * CW, i * BLK : (i + 1) * BLK])
        for u in range(UNROLL):
            r = row_of(base + u)
            pre[r] = terms[u] if u < stored else pre[r] + terms[u]
        return c

    gather(0, 0, ROWB)
    lax.fori_loop(1, MAXB // UNROLL, gather, 0)

    for r in range(ROWB):
        v = pre[r]
        at = slice(r * BLK, (r + 1) * BLK)
        sigma = jax.nn.sigmoid(v)
        act[:, at] = (v * sigma).astype(jnp.bfloat16)
        gpre[r] = (cot[:, at].astype(jnp.float32) * sigma * (1.0 + v * (1.0 - sigma))).astype(
            jnp.bfloat16
        )
    gpre[ROWB] = jnp.zeros((CW, BLK), jnp.bfloat16)

    def spread(j, c, stored=0):
        base = j * UNROLL
        terms = []
        for b in [base + u for u in range(0, UNROLL, 2)]:
            rows = jnp.concatenate([gpre[row_of(b)], gpre[row_of(b + 1)]], axis=0)
            pair = jnp.dot(
                rows,
                jnp.concatenate([held[b], held[b + 1]], axis=1),
                preferred_element_type=jnp.float32,
            )
            terms += [pair[:CW, :BLK], pair[CW:, BLK:]]
        for u in range(UNROLL):
            col = coords[1, base + u]
            grad[col] = terms[u] if u < stored else grad[col] + terms[u]
        return c

    spread(0, 0, COLB)
    lax.fori_loop(1, MAXB // UNROLL, spread, 0)
    for g in range(GP):
        for s in range(2):
            at = slice(s * BLK, (s + 1) * BLK)
            local[g, :, at] = grad[2 * g + s]
            remote[g, :, at] = grad[ROWB + 2 * g + s].astype(jnp.bfloat16)


def blocks(coords, counts, adjacency, own, halo, cotangent):
    return pl.pallas_call(
        blocks_kernel,
        out_shape=(
            jax.ShapeDtypeStruct((CW, ROWB * BLK), jnp.bfloat16),
            jax.ShapeDtypeStruct((GP, CW, LO), jnp.float32),
            jax.ShapeDtypeStruct((NN, CW, HP), jnp.bfloat16),
        ),
        in_specs=[
            pl.BlockSpec(memory_space=VMEM),
            pl.BlockSpec(memory_space=pltpu.SMEM),
            pl.BlockSpec(memory_space=VMEM),
            pl.BlockSpec(memory_space=VMEM),
            pl.BlockSpec(memory_space=VMEM),
            pl.BlockSpec(memory_space=VMEM),
        ],
        out_specs=(pl.BlockSpec(memory_space=VMEM),) * 3,
        scratch_shapes=[
            pltpu.SMEM((2, MAXB), jnp.int32),
            VMEM((COLB, CW, BLK), jnp.bfloat16),
            VMEM((ROWB + 1, CW, BLK), jnp.float32),
            VMEM((ROWB + 1, CW, BLK), jnp.bfloat16),
            VMEM((COLB, CW, BLK), jnp.float32),
            pltpu.SemaphoreType.DMA,
        ],
        compiler_params=pltpu.CompilerParams(vmem_limit_bytes=14 * 2**20),
        name="blocks",
    )(coords, counts, adjacency, own, halo, cotangent)


def backward_kernel(
    remote, local, lists, xs, w_ref, in_grad, w_grad,
    wt, x_far, x_other, landed, acc, gz, gz_rows, pieces, pland, zpart, zland, whole,
    nsend, nrecv, fsend, frecv, xsend, xrecv, osend, orecv, psend, precv, zsend, zrecv, asend, arecv,
):
    n = lax.axis_index("node")
    f = lax.axis_index("feat")
    y = lax.shift_right_logical(f, 1)
    core = f & 1
    far = y ^ 2
    barrier = enter(n, f)

    def add(lists_at, vals):
        hots = [one_hot_t(lists, p) for p in lists_at]
        hot = jnp.concatenate([h for h, _ in hots], axis=1)
        step = 8
        for g in range(0, GP, step):
            rows = jnp.concatenate(
                [
                    jnp.concatenate(
                        [jnp.where(hi == g + h, v, 0.0).astype(jnp.bfloat16) for h in range(step)],
                        axis=0,
                    )
                    for (_, hi), v in zip(hots, vals)
                ],
                axis=1,
            )
            term = lax.dot_general(rows, hot, NT, preferred_element_type=jnp.float32)
            acc[g : g + step] = acc[g : g + step] + term.reshape(step, CW, LO)

    pl.semaphore_wait(barrier, NN + NF - 2)

    def node_copy(k, to, source):
        return pltpu.make_async_remote_copy(
            src_ref=remote.at[to],
            dst_ref=landed.at[source],
            send_sem=nsend.at[k],
            recv_sem=nrecv.at[k],
            device_id={"node": to},
            device_id_type=MESH,
        )

    for k in range(1, XS):
        node_copy(k, node_at(n, k), n).start()

    def start_nodes(i, c):
        for j in range(XS):
            k = far_first(i) * XS + j
            node_copy(k, node_at(n, k), n).start()
        return c

    lax.fori_loop(0, ZS - 1, start_nodes, 0)
    far_copy = pltpu.make_async_remote_copy(
        src_ref=xs.at[y],
        dst_ref=x_far,
        send_sem=xsend,
        recv_sem=xrecv,
        device_id={"feat": f ^ 4},
        device_id_type=MESH,
    )

    def other_copy(k, src):
        return pltpu.make_async_remote_copy(
            src_ref=src,
            dst_ref=x_other.at[(y + k) & (NY - 1)],
            send_sem=osend.at[k],
            recv_sem=orecv.at[k],
            device_id={"feat": f ^ 1},
            device_id_type=MESH,
        )

    far_copy.start()
    for k in (0, 1, 3):
        other_copy(k, xs.at[(y + k) & (NY - 1)]).start()
    wt[...] = w_ref[...].astype(jnp.float32).T.astype(jnp.bfloat16)
    acc[...] = local[...]
    sources = [node_back(n, k) for k in range(XS)]
    for k in range(1, XS):
        node_copy(k, node_at(n, k), sources[k]).wait_recv()
    landed[n] = remote[n]
    add(sources, [landed[p].astype(jnp.float32) for p in sources])

    def take_nodes(i, c):
        ks = [far_first(i) * XS + j for j in range(XS)]
        sources = [node_back(n, k) for k in ks]
        for k, p in zip(ks, sources):
            node_copy(k, node_at(n, k), p).wait_recv()
        add(sources, [landed[p].astype(jnp.float32) for p in sources])
        return c

    lax.fori_loop(0, ZS - 4, take_nodes, 0)
    far_copy.wait_recv()
    other_copy(2, x_far).start()
    lax.fori_loop(ZS - 4, ZS - 1, take_nodes, 0)
    gz[...] = acc[...].astype(jnp.bfloat16)

    def feat_copy(k, to, source):
        return pltpu.make_async_remote_copy(
            src_ref=gz.at[pl.ds(to * GD, GD)],
            dst_ref=gz_rows.at[:, pl.ds(pl.multiple_of(source * CW, CW), CW), :],
            send_sem=fsend.at[k],
            recv_sem=frecv.at[k],
            device_id={"feat": to},
            device_id_type=MESH,
        )

    def start_feat(k, c):
        feat_copy(k, feat_at(f, k), f).start()
        return c

    lax.fori_loop(1, NF, start_feat, 0)
    for k in range(NY):
        other_copy(k, x_far).wait_recv()

    def product(rows, at, group):
        out = jnp.zeros((CW, F), jnp.float32)
        for j in range(GD):
            out = out + jnp.dot(
                gz[group + j],
                rows[at, j * LO : (j + 1) * LO, :],
                preferred_element_type=jnp.float32,
            )
        return out

    mine = product(x_far.reshape(1, RD, F), 0, GD * (2 * far + core))
    for k in (0, 1, 3):
        at = (y + k) & (NY - 1)
        mine = mine + product(xs, at, GD * (2 * at + core))
    for at in range(NY):
        mine = mine + product(x_other, at, GD * (2 * at + 1 - core))
    mine = mine * (1.0 / math.sqrt(NN * ROWB * BLK))
    z, x = n & -XS, n & (XS - 1)
    pieces[...] = mine.reshape(XS, CW // XS, F)

    def x_at(k):
        return z + ((x + k) & (XS - 1))

    def z_at(k):
        return ((z + XS * k) & (NN - 1)) + x

    def share_copy(k, source):
        to = x_at(k)
        return pltpu.make_async_remote_copy(
            src_ref=pieces.at[to & (XS - 1)],
            dst_ref=pland.at[source & (XS - 1)],
            send_sem=psend.at[k],
            recv_sem=precv.at[k],
            device_id={"node": to},
            device_id_type=MESH,
        )

    for k in range(1, XS):
        share_copy(k, n).start()
    pland[x] = pieces[x]
    for k in range(1, XS):
        share_copy(k, x_at(XS - k)).wait_recv()
    zpart[...] = pland[0] + pland[1] + pland[2] + pland[3]

    def z_copy(k, source):
        return pltpu.make_async_remote_copy(
            src_ref=zpart,
            dst_ref=zland.at[lax.shift_right_logical(source, 2)],
            send_sem=zsend.at[k],
            recv_sem=zrecv.at[k],
            device_id={"node": z_at(k)},
            device_id_type=MESH,
        )

    for k in range(1, ZS):
        z_copy(k, n).start()

    zland[lax.shift_right_logical(n, 2)] = zpart[...]
    for k in range(1, ZS):
        z_copy(k, z_at(ZS - k)).wait_recv()
    summed = zland[0]
    for i in range(1, ZS):
        summed = summed + zland[i]
    whole[x] = summed

    def back_copy(k, source):
        return pltpu.make_async_remote_copy(
            src_ref=whole.at[x],
            dst_ref=whole.at[source & (XS - 1)],
            send_sem=asend.at[k],
            recv_sem=arecv.at[k],
            device_id={"node": x_at(k)},
            device_id_type=MESH,
        )

    for k in range(1, XS):
        back_copy(k, n).start()

    gz_rows[:, pl.ds(pl.multiple_of(f * CW, CW), CW), :] = gz[pl.ds(f * GD, GD)]

    def wait_feat(k, c):
        feat_copy(k, feat_at(f, k), feat_back(f, k)).wait_recv()
        return c

    lax.fori_loop(1, NF, wait_feat, 0)
    for h in range(GD):
        rows = gz_rows[h].astype(jnp.float32).T.astype(jnp.bfloat16)
        in_grad[h * LO : (h + 1) * LO, :] = jnp.dot(
            rows, wt[...], preferred_element_type=jnp.float32
        ).astype(jnp.bfloat16)

    for k in range(1, XS):
        back_copy(k, x_at(XS - k)).wait_recv()
    w_grad[...] = whole[...].reshape(CW, F)
    for k in range(1, XS):
        share_copy(k, n).wait_send()
        back_copy(k, n).wait_send()
    for k in range(1, ZS):
        z_copy(k, n).wait_send()

    def finish_node(k, c):
        node_copy(k, node_at(n, k), n).wait_send()
        return c

    lax.fori_loop(1, NN, finish_node, 0)

    def finish_feat(k, c):
        feat_copy(k, feat_at(f, k), f).wait_send()
        return c

    lax.fori_loop(1, NF, finish_feat, 0)
    far_copy.wait_send()
    for k in range(NY):
        other_copy(k, x_far).wait_send()


def backward(remote, local, lists, xs, weight):
    dma = pltpu.SemaphoreType.DMA
    return pl.pallas_call(
        backward_kernel,
        out_shape=(
            jax.ShapeDtypeStruct((RD, F), jnp.bfloat16),
            jax.ShapeDtypeStruct((CW, F), jnp.float32),
        ),
        in_specs=[
            pl.BlockSpec(memory_space=VMEM),
            pl.BlockSpec(memory_space=VMEM),
            pl.BlockSpec(memory_space=VMEM),
            pl.BlockSpec(memory_space=VMEM),
            pl.BlockSpec(memory_space=VMEM),
        ],
        out_specs=(pl.BlockSpec(memory_space=VMEM),) * 2,
        scratch_shapes=[
            VMEM((F, F), jnp.bfloat16),
            VMEM((RD, F), jnp.bfloat16),
            VMEM((NY, RD, F), jnp.bfloat16),
            VMEM((NN, CW, HP), jnp.bfloat16),
            VMEM((GP, CW, LO), jnp.float32),
            VMEM((GP, CW, LO), jnp.bfloat16),
            VMEM((GD, F, LO), jnp.bfloat16),
            VMEM((XS, CW // XS, F), jnp.float32),
            VMEM((XS, CW // XS, F), jnp.float32),
            VMEM((CW // XS, F), jnp.float32),
            VMEM((ZS, CW // XS, F), jnp.float32),
            VMEM((XS, CW // XS, F), jnp.float32),
            dma((NN,)),
            dma((NN,)),
            dma((NF,)),
            dma((NF,)),
            dma,
            dma,
            dma((NY,)),
            dma((NY,)),
            dma((XS,)),
            dma((XS,)),
            dma((ZS,)),
            dma((ZS,)),
            dma((XS,)),
            dma((XS,)),
        ],
        compiler_params=pltpu.CompilerParams(
            collective_id=1, has_side_effects=True, vmem_limit_bytes=32 * 2**20
        ),
        name="return_and_sum",
    )(remote, local, lists, xs, weight)


def body(features, weight, adjacency, block_coords, block_counts, send_rows, cotangent):
    own, halo, xs, held, cot, coords = forward(
        features, weight, send_rows, adjacency, cotangent, block_coords
    )
    activations, local, remote = blocks(coords, block_counts, held, own, halo, cot)
    input_grad, weight_grad_t = backward(remote, local, send_rows, xs, weight)
    weight_grad = weight_grad_t.T
    return (activations, input_grad, weight_grad)


def solution(mesh):
    return jax.shard_map(
        body,
        mesh=mesh,
        in_specs=(
            P(("node", "feat"), None),
            P(),
            P("node", None, None),
            P(None, "node"),
            P("node"),
            P("node", None),
            P("feat", "node"),
        ),
        out_specs=(P("feat", "node"), P(("node", "feat"), None), P(None, "feat")),
        check_vma=False,
    )
```

```python
import functools
import math

import jax
import jax.numpy as jnp
from jax import lax
from jax.experimental import pallas as pl
from jax.experimental.pallas import tpu as pltpu
from jax.sharding import PartitionSpec as P

ZS, XS = 8, 4
NN = ZS * XS
NF = 8
NY = 4
F = 256
CW = F // NF
RD = 1024
LO = 256
GD = RD // LO
GP = NF * GD
HP = 256
BLK = 128
NT = (((1,), (1,)), ((), ()))
ROWB = 64
COLB = 128
MAXB = 512
MESH = pl.DeviceIdType.MESH
VMEM = pltpu.VMEM


def node_at(n, k):
    z = ((n & -XS) + (k & -XS)) & (NN - 1)
    x = (n + k) & (XS - 1)
    return z + x


def node_back(n, k):
    z = ((n & -XS) + NN - (k & -XS)) & (NN - 1)
    x = (n + XS - (k & (XS - 1))) & (XS - 1)
    return z + x


def far_first(i):
    return ZS // 2 + (i // 2) * (1 - (i & 1)) - ((i + 1) // 2) * (i & 1)


def feat_at(f, k):
    return (f + k) & (NF - 1)


def feat_back(f, k):
    return (f + NF - k) & (NF - 1)


def enter(n, f):
    barrier = pltpu.get_barrier_semaphore()

    for k in range(1, NF):
        pl.semaphore_signal(barrier, inc=1, device_id={"feat": feat_at(f, k)}, device_id_type=MESH)
    for k in range(1, NN):
        pl.semaphore_signal(barrier, inc=1, device_id={"node": node_at(n, k)}, device_id_type=MESH)
    return barrier


def one_hot_t(lists, p):
    idx = lists[pl.ds(p, 1), :]
    lo = idx & (LO - 1)
    hi = lax.shift_right_logical(idx, 8)
    rows = lax.broadcasted_iota(jnp.int32, (LO, HP), 0)
    return (rows == lo).astype(jnp.float32).astype(jnp.bfloat16), hi


def forward_kernel(
    x_hbm, w_hbm, lists_hbm, adj_hbm, cot_hbm, coords_hbm,
    own, halo, xs, adj, cot, coords,
    w_ref, lists, proj, packed, fsend, frecv, nsend, nrecv, xsend, xrecv, lsem,
):
    n = lax.axis_index("node")
    f = lax.axis_index("feat")
    y = lax.shift_right_logical(f, 1)
    x_ref = xs.at[y]
    loads = [
        pltpu.make_async_copy(src, dst, lsem.at[i])
        for i, (src, dst) in enumerate(
            [
                (x_hbm, x_ref),
                (w_hbm, w_ref),
                (lists_hbm, lists),
                (coords_hbm, coords),
                (cot_hbm, cot),
                (adj_hbm, adj),
            ]
        )
    ]
    for load in loads:
        load.start()
    barrier = enter(n, f)
    loads[0].wait()
    loads[1].wait()
    wt = w_ref[...].astype(jnp.float32).T.astype(jnp.bfloat16)
    for h in range(GD):
        proj[h] = lax.dot_general(
            wt,
            xs[y, h * LO : (h + 1) * LO, :],
            (((1,), (1,)), ((), ())),
            preferred_element_type=jnp.float32,
        ).astype(jnp.bfloat16)
    pl.semaphore_wait(barrier, NN + NF - 2)

    def feat_copy(k, to, source):
        return pltpu.make_async_remote_copy(
            src_ref=proj.at[:, pl.ds(pl.multiple_of(to * CW, CW), CW), :],
            dst_ref=own.at[pl.ds(source * GD, GD)],
            send_sem=fsend.at[k],
            recv_sem=frecv.at[k],
            device_id={"feat": to},
            device_id_type=MESH,
        )

    def start_feat(k, c):
        feat_copy(k, feat_at(f, k), f).start()
        return c

    lax.fori_loop(1, NF, start_feat, 0)
    loads[2].wait()
    own[pl.ds(f * GD, GD)] = proj[:, pl.ds(pl.multiple_of(f * CW, CW), CW), :]

    def wait_feat(k, c):
        feat_copy(k, feat_at(f, k), feat_back(f, k)).wait_recv()
        return c

    lax.fori_loop(1, NF, wait_feat, 0)

    def rows_copy(k, source):
        return pltpu.make_async_remote_copy(
            src_ref=xs.at[y],
            dst_ref=xs.at[source],
            send_sem=xsend.at[k],
            recv_sem=xrecv.at[k],
            device_id={"feat": feat_at(f, 2 * k)},
            device_id_type=MESH,
        )

    for k in (1, 3):
        rows_copy(k, y).start()

    def pick(lists_at):
        hots = [one_hot_t(lists, p) for p in lists_at]
        hot = jnp.concatenate([h for h, _ in hots], axis=1)
        hi = jnp.concatenate([h for _, h in hots], axis=1)
        got = jnp.zeros((CW, len(hots) * HP), jnp.float32)
        step = 8
        for g in range(0, GP, step):
            part = jnp.dot(
                own[g : g + step].reshape(step * CW, LO), hot, preferred_element_type=jnp.float32
            )
            for h in range(step):
                got = jnp.where(hi == g + h, part[h * CW : (h + 1) * CW], got)
        got = got.astype(jnp.bfloat16)
        return [got[:, i * HP : (i + 1) * HP] for i in range(len(hots))]

    def node_copy(k, to, source):
        return pltpu.make_async_remote_copy(
            src_ref=packed.at[k],
            dst_ref=halo.at[source],
            send_sem=nsend.at[k],
            recv_sem=nrecv.at[k],
            device_id={"node": to},
            device_id_type=MESH,
        )

    def send_some(ks):
        tos = [node_at(n, k) for k in ks]
        for k, to, got in zip(ks, tos, pick(tos)):
            packed[k] = got
            node_copy(k, to, n).start()

    def send_nodes(i, c):
        send_some([far_first(i) * XS + j for j in range(XS)])
        return c

    first = far_first(0) * XS
    send_some([first])
    send_some([first + j for j in range(1, XS)])
    lax.fori_loop(1, ZS - 1, send_nodes, 0)
    tos = [node_at(n, k) for k in range(XS)]
    for k, (to, got) in enumerate(zip(tos, pick(tos))):
        if k == 0:
            halo[n] = got
        else:
            packed[k] = got
            node_copy(k, to, n).start()

    def finish_node(i, c):
        k = NN - i
        node_copy(k, node_at(n, k), node_back(n, k)).wait()
        return c

    lax.fori_loop(1, NN, finish_node, 0)

    def finish_feat(k, c):
        feat_copy(k, feat_at(f, k), f).wait_send()
        return c

    lax.fori_loop(1, NF, finish_feat, 0)
    for k in (1, 3):
        rows_copy(k, (y + NY - k) & (NY - 1)).wait()
    for load in loads[3:]:
        load.wait()


def forward(features, weight, lists, adjacency, cotangent, coords):
    part = jax.ShapeDtypeStruct((GP, CW, LO), jnp.bfloat16)

    def like(a):
        return jax.ShapeDtypeStruct(a.shape, a.dtype)

    return pl.pallas_call(
        forward_kernel,
        out_shape=(
            part,
            part,
            jax.ShapeDtypeStruct((NY, RD, F), jnp.bfloat16),
            like(adjacency),
            like(cotangent),
            like(coords),
        ),
        in_specs=[pl.BlockSpec(memory_space=pltpu.HBM)] * 6,
        out_specs=(pl.BlockSpec(memory_space=VMEM),) * 6,
        scratch_shapes=[
            VMEM((F, F), jnp.bfloat16),
            VMEM((NN, HP), jnp.int32),
            VMEM((GD, F, LO), jnp.bfloat16),
            VMEM((NN, CW, HP), jnp.bfloat16),
            pltpu.SemaphoreType.DMA((NF,)),
            pltpu.SemaphoreType.DMA((NF,)),
            pltpu.SemaphoreType.DMA((NN,)),
            pltpu.SemaphoreType.DMA((NN,)),
            pltpu.SemaphoreType.DMA((NY,)),
            pltpu.SemaphoreType.DMA((NY,)),
            pltpu.SemaphoreType.DMA((6,)),
        ],
        compiler_params=pltpu.CompilerParams(
            collective_id=0, has_side_effects=True, vmem_limit_bytes=12 * 2**20
        ),
        name="project_and_send",
    )(
        *(
            pltpu.with_memory_space_constraint(a, pltpu.HBM)
            for a in (features, weight, lists, adjacency, cotangent, coords)
        )
    )


UNROLL = 256
WIDE = 4


def blocks_kernel(
    coords_v, counts, held, own, halo, cot, act, local, remote, coords, ext, pre, gpre, grad, sem
):
    load = pltpu.make_async_copy(coords_v, coords, sem)
    load.start()
    count = counts[0]
    pre[ROWB] = jnp.zeros((CW, BLK), jnp.float32)
    for g in range(GP):
        for s in range(2):
            ext[2 * g + s] = own[g, :, s * BLK : (s + 1) * BLK]
            ext[ROWB + 2 * g + s] = halo[g, :, s * BLK : (s + 1) * BLK]
    load.wait()

    def row_of(b):
        return jnp.where(b < count, coords[0, b], ROWB)

    def gather(j, c, stored=0):
        base = j * UNROLL
        terms = []
        for b in [base + u for u in range(0, UNROLL, WIDE)]:
            cols = jnp.concatenate([ext[coords[1, b + i]] for i in range(WIDE)], axis=0)
            part = lax.dot_general(
                cols,
                held[pl.ds(b, WIDE)].reshape(WIDE * BLK, BLK),
                NT,
                preferred_element_type=jnp.float32,
            )
            for i in range(WIDE):
                terms.append(part[i * CW : (i + 1) * CW, i * BLK : (i + 1) * BLK])
        for u in range(UNROLL):
            r = row_of(base + u)
            pre[r] = terms[u] if u < stored else pre[r] + terms[u]
        return c

    gather(0, 0, ROWB)
    lax.fori_loop(1, MAXB // UNROLL, gather, 0)

    for r in range(ROWB):
        v = pre[r]
        at = slice(r * BLK, (r + 1) * BLK)
        sigma = jax.nn.sigmoid(v)
        act[:, at] = (v * sigma).astype(jnp.bfloat16)
        gpre[r] = (cot[:, at].astype(jnp.float32) * sigma * (1.0 + v * (1.0 - sigma))).astype(
            jnp.bfloat16
        )
    gpre[ROWB] = jnp.zeros((CW, BLK), jnp.bfloat16)

    def spread(j, c, stored=0):
        base = j * UNROLL
        terms = []
        for b in [base + u for u in range(0, UNROLL, 2)]:
            rows = jnp.concatenate([gpre[row_of(b)], gpre[row_of(b + 1)]], axis=0)
            pair = jnp.dot(
                rows,
                jnp.concatenate([held[b], held[b + 1]], axis=1),
                preferred_element_type=jnp.float32,
            )
            terms += [pair[:CW, :BLK], pair[CW:, BLK:]]
        for u in range(UNROLL):
            col = coords[1, base + u]
            grad[col] = terms[u] if u < stored else grad[col] + terms[u]
        return c

    spread(0, 0, COLB)
    lax.fori_loop(1, MAXB // UNROLL, spread, 0)
    for g in range(GP):
        for s in range(2):
            at = slice(s * BLK, (s + 1) * BLK)
            local[g, :, at] = grad[2 * g + s]
            remote[g, :, at] = grad[ROWB + 2 * g + s].astype(jnp.bfloat16)


def blocks(coords, counts, adjacency, own, halo, cotangent):
    return pl.pallas_call(
        blocks_kernel,
        out_shape=(
            jax.ShapeDtypeStruct((CW, ROWB * BLK), jnp.bfloat16),
            jax.ShapeDtypeStruct((GP, CW, LO), jnp.float32),
            jax.ShapeDtypeStruct((NN, CW, HP), jnp.bfloat16),
        ),
        in_specs=[
            pl.BlockSpec(memory_space=VMEM),
            pl.BlockSpec(memory_space=pltpu.SMEM),
            pl.BlockSpec(memory_space=VMEM),
            pl.BlockSpec(memory_space=VMEM),
            pl.BlockSpec(memory_space=VMEM),
            pl.BlockSpec(memory_space=VMEM),
        ],
        out_specs=(pl.BlockSpec(memory_space=VMEM),) * 3,
        scratch_shapes=[
            pltpu.SMEM((2, MAXB), jnp.int32),
            VMEM((COLB, CW, BLK), jnp.bfloat16),
            VMEM((ROWB + 1, CW, BLK), jnp.float32),
            VMEM((ROWB + 1, CW, BLK), jnp.bfloat16),
            VMEM((COLB, CW, BLK), jnp.float32),
            pltpu.SemaphoreType.DMA,
        ],
        compiler_params=pltpu.CompilerParams(vmem_limit_bytes=14 * 2**20),
        name="blocks",
    )(coords, counts, adjacency, own, halo, cotangent)


def backward_kernel(
    remote, local, lists, xs, w_ref, in_grad, w_grad,
    wt, x_far, x_other, landed, acc, gz, gz_rows, pieces, pland, zpart, zland, whole,
    nsend, nrecv, fsend, frecv, xsend, xrecv, osend, orecv, psend, precv, zsend, zrecv, asend, arecv,
):
    n = lax.axis_index("node")
    f = lax.axis_index("feat")
    y = lax.shift_right_logical(f, 1)
    core = f & 1
    far = y ^ 2
    barrier = enter(n, f)

    def add(lists_at, vals):
        hots = [one_hot_t(lists, p) for p in lists_at]
        hot = jnp.concatenate([h for h, _ in hots], axis=1)
        step = 8
        for g in range(0, GP, step):
            rows = jnp.concatenate(
                [
                    jnp.concatenate(
                        [jnp.where(hi == g + h, v, 0.0).astype(jnp.bfloat16) for h in range(step)],
                        axis=0,
                    )
                    for (_, hi), v in zip(hots, vals)
                ],
                axis=1,
            )
            term = lax.dot_general(rows, hot, NT, preferred_element_type=jnp.float32)
            acc[g : g + step] = acc[g : g + step] + term.reshape(step, CW, LO)

    pl.semaphore_wait(barrier, NN + NF - 2)

    def node_copy(k, to, source):
        return pltpu.make_async_remote_copy(
            src_ref=remote.at[to],
            dst_ref=landed.at[source],
            send_sem=nsend.at[k],
            recv_sem=nrecv.at[k],
            device_id={"node": to},
            device_id_type=MESH,
        )

    for k in range(1, XS):
        node_copy(k, node_at(n, k), n).start()

    def start_nodes(i, c):
        for j in range(XS):
            k = far_first(i) * XS + j
            node_copy(k, node_at(n, k), n).start()
        return c

    lax.fori_loop(0, ZS - 1, start_nodes, 0)
    far_copy = pltpu.make_async_remote_copy(
        src_ref=xs.at[y],
        dst_ref=x_far,
        send_sem=xsend,
        recv_sem=xrecv,
        device_id={"feat": f ^ 4},
        device_id_type=MESH,
    )

    def other_copy(k, src):
        return pltpu.make_async_remote_copy(
            src_ref=src,
            dst_ref=x_other.at[(y + k) & (NY - 1)],
            send_sem=osend.at[k],
            recv_sem=orecv.at[k],
            device_id={"feat": f ^ 1},
            device_id_type=MESH,
        )

    far_copy.start()
    for k in (0, 1, 3):
        other_copy(k, xs.at[(y + k) & (NY - 1)]).start()
    wt[...] = w_ref[...].astype(jnp.float32).T.astype(jnp.bfloat16)
    acc[...] = local[...]
    sources = [node_back(n, k) for k in range(XS)]
    for k in range(1, XS):
        node_copy(k, node_at(n, k), sources[k]).wait_recv()
    landed[n] = remote[n]
    add(sources, [landed[p].astype(jnp.float32) for p in sources])

    def take_nodes(i, c):
        ks = [far_first(i) * XS + j for j in range(XS)]
        sources = [node_back(n, k) for k in ks]
        for k, p in zip(ks, sources):
            node_copy(k, node_at(n, k), p).wait_recv()
        add(sources, [landed[p].astype(jnp.float32) for p in sources])
        return c

    lax.fori_loop(0, ZS - 4, take_nodes, 0)
    far_copy.wait_recv()
    other_copy(2, x_far).start()
    lax.fori_loop(ZS - 4, ZS - 1, take_nodes, 0)
    gz[...] = acc[...].astype(jnp.bfloat16)

    def feat_copy(k, to, source):
        return pltpu.make_async_remote_copy(
            src_ref=gz.at[pl.ds(to * GD, GD)],
            dst_ref=gz_rows.at[:, pl.ds(pl.multiple_of(source * CW, CW), CW), :],
            send_sem=fsend.at[k],
            recv_sem=frecv.at[k],
            device_id={"feat": to},
            device_id_type=MESH,
        )

    def start_feat(k, c):
        feat_copy(k, feat_at(f, k), f).start()
        return c

    lax.fori_loop(1, NF, start_feat, 0)
    for k in range(NY):
        other_copy(k, x_far).wait_recv()

    def product(rows, at, group):
        out = jnp.zeros((CW, F), jnp.float32)
        for j in range(GD):
            out = out + jnp.dot(
                gz[group + j],
                rows[at, j * LO : (j + 1) * LO, :],
                preferred_element_type=jnp.float32,
            )
        return out

    mine = product(x_far.reshape(1, RD, F), 0, GD * (2 * far + core))
    for k in (0, 1, 3):
        at = (y + k) & (NY - 1)
        mine = mine + product(xs, at, GD * (2 * at + core))
    for at in range(NY):
        mine = mine + product(x_other, at, GD * (2 * at + 1 - core))
    mine = mine * (1.0 / math.sqrt(NN * ROWB * BLK))
    z, x = n & -XS, n & (XS - 1)
    pieces[...] = mine.reshape(XS, CW // XS, F)

    def x_at(k):
        return z + ((x + k) & (XS - 1))

    def z_at(k):
        return ((z + XS * k) & (NN - 1)) + x

    def share_copy(k, source):
        to = x_at(k)
        return pltpu.make_async_remote_copy(
            src_ref=pieces.at[to & (XS - 1)],
            dst_ref=pland.at[source & (XS - 1)],
            send_sem=psend.at[k],
            recv_sem=precv.at[k],
            device_id={"node": to},
            device_id_type=MESH,
        )

    for k in range(1, XS):
        share_copy(k, n).start()
    pland[x] = pieces[x]
    for k in range(1, XS):
        share_copy(k, x_at(XS - k)).wait_recv()
    zpart[...] = pland[0] + pland[1] + pland[2] + pland[3]

    def z_copy(k, source):
        return pltpu.make_async_remote_copy(
            src_ref=zpart,
            dst_ref=zland.at[lax.shift_right_logical(source, 2)],
            send_sem=zsend.at[k],
            recv_sem=zrecv.at[k],
            device_id={"node": z_at(k)},
            device_id_type=MESH,
        )

    for k in range(1, ZS):
        z_copy(k, n).start()

    zland[lax.shift_right_logical(n, 2)] = zpart[...]
    for k in range(1, ZS):
        z_copy(k, z_at(ZS - k)).wait_recv()
    summed = zland[0]
    for i in range(1, ZS):
        summed = summed + zland[i]
    whole[x] = summed

    def back_copy(k, source):
        return pltpu.make_async_remote_copy(
            src_ref=whole.at[x],
            dst_ref=whole.at[source & (XS - 1)],
            send_sem=asend.at[k],
            recv_sem=arecv.at[k],
            device_id={"node": x_at(k)},
            device_id_type=MESH,
        )

    for k in range(1, XS):
        back_copy(k, n).start()

    gz_rows[:, pl.ds(pl.multiple_of(f * CW, CW), CW), :] = gz[pl.ds(f * GD, GD)]

    def wait_feat(k, c):
        feat_copy(k, feat_at(f, k), feat_back(f, k)).wait_recv()
        return c

    lax.fori_loop(1, NF, wait_feat, 0)
    for h in range(GD):
        rows = gz_rows[h].astype(jnp.float32).T.astype(jnp.bfloat16)
        in_grad[h * LO : (h + 1) * LO, :] = jnp.dot(
            rows, wt[...], preferred_element_type=jnp.float32
        ).astype(jnp.bfloat16)

    for k in range(1, XS):
        back_copy(k, x_at(XS - k)).wait_recv()
    w_grad[...] = whole[...].reshape(CW, F)
    for k in range(1, XS):
        share_copy(k, n).wait_send()
        back_copy(k, n).wait_send()
    for k in range(1, ZS):
        z_copy(k, n).wait_send()

    def finish_node(k, c):
        node_copy(k, node_at(n, k), n).wait_send()
        return c

    lax.fori_loop(1, NN, finish_node, 0)

    def finish_feat(k, c):
        feat_copy(k, feat_at(f, k), f).wait_send()
        return c

    lax.fori_loop(1, NF, finish_feat, 0)
    far_copy.wait_send()
    for k in range(NY):
        other_copy(k, x_far).wait_send()


def backward(remote, local, lists, xs, weight):
    dma = pltpu.SemaphoreType.DMA
    return pl.pallas_call(
        backward_kernel,
        out_shape=(
            jax.ShapeDtypeStruct((RD, F), jnp.bfloat16),
            jax.ShapeDtypeStruct((CW, F), jnp.float32),
        ),
        in_specs=[
            pl.BlockSpec(memory_space=VMEM),
            pl.BlockSpec(memory_space=VMEM),
            pl.BlockSpec(memory_space=VMEM),
            pl.BlockSpec(memory_space=VMEM),
            pl.BlockSpec(memory_space=VMEM),
        ],
        out_specs=(pl.BlockSpec(memory_space=VMEM),) * 2,
        scratch_shapes=[
            VMEM((F, F), jnp.bfloat16),
            VMEM((RD, F), jnp.bfloat16),
            VMEM((NY, RD, F), jnp.bfloat16),
            VMEM((NN, CW, HP), jnp.bfloat16),
            VMEM((GP, CW, LO), jnp.float32),
            VMEM((GP, CW, LO), jnp.bfloat16),
            VMEM((GD, F, LO), jnp.bfloat16),
            VMEM((XS, CW // XS, F), jnp.float32),
            VMEM((XS, CW // XS, F), jnp.float32),
            VMEM((CW // XS, F), jnp.float32),
            VMEM((ZS, CW // XS, F), jnp.float32),
            VMEM((XS, CW // XS, F), jnp.float32),
            dma((NN,)),
            dma((NN,)),
            dma((NF,)),
            dma((NF,)),
            dma,
            dma,
            dma((NY,)),
            dma((NY,)),
            dma((XS,)),
            dma((XS,)),
            dma((ZS,)),
            dma((ZS,)),
            dma((XS,)),
            dma((XS,)),
        ],
        compiler_params=pltpu.CompilerParams(
            collective_id=1, has_side_effects=True, vmem_limit_bytes=32 * 2**20
        ),
        name="return_and_sum",
    )(remote, local, lists, xs, weight)


def body(features, weight, adjacency, block_coords, block_counts, send_rows, cotangent):
    own, halo, xs, held, cot, coords = forward(
        features, weight, send_rows, adjacency, cotangent, block_coords
    )
    activations, local, remote = blocks(coords, block_counts, held, own, halo, cot)
    input_grad, weight_grad_t = backward(remote, local, send_rows, xs, weight)
    weight_grad = weight_grad_t.T
    return (activations, input_grad, weight_grad)


def solution(mesh):
    return jax.shard_map(
        body,
        mesh=mesh,
        in_specs=(
            P(("node", "feat"), None),
            P(),
            P("node", None, None),
            P(None, "node"),
            P("node"),
            P("node", None),
            P("feat", "node"),
        ),
        out_specs=(P("feat", "node"), P(("node", "feat"), None), P(None, "feat")),
        check_vma=False,
    )
```

```python
import functools
import math

import jax
import jax.numpy as jnp
from jax import lax
from jax.experimental import pallas as pl
from jax.experimental.pallas import tpu as pltpu
from jax.sharding import PartitionSpec as P

ZS, XS = 8, 4
NN = ZS * XS
NF = 8
NY = 4
F = 256
CW = F // NF
RD = 1024
LO = 256
GD = RD // LO
GP = NF * GD
HP = 256
BLK = 128
NT = (((1,), (1,)), ((), ()))
ROWB = 64
COLB = 128
MAXB = 512
MESH = pl.DeviceIdType.MESH
VMEM = pltpu.VMEM


def node_at(n, k):
    z = ((n & -XS) + (k & -XS)) & (NN - 1)
    x = (n + k) & (XS - 1)
    return z + x


def node_back(n, k):
    z = ((n & -XS) + NN - (k & -XS)) & (NN - 1)
    x = (n + XS - (k & (XS - 1))) & (XS - 1)
    return z + x


def far_first(i):
    return ZS // 2 + (i // 2) * (1 - (i & 1)) - ((i + 1) // 2) * (i & 1)


def feat_at(f, k):
    return (f + k) & (NF - 1)


def feat_back(f, k):
    return (f + NF - k) & (NF - 1)


def enter(n, f):
    barrier = pltpu.get_barrier_semaphore()

    for k in range(1, NF):
        pl.semaphore_signal(barrier, inc=1, device_id={"feat": feat_at(f, k)}, device_id_type=MESH)
    for k in range(1, NN):
        pl.semaphore_signal(barrier, inc=1, device_id={"node": node_at(n, k)}, device_id_type=MESH)
    return barrier


def one_hot_t(lists, p):
    idx = lists[pl.ds(p, 1), :]
    lo = idx & (LO - 1)
    hi = lax.shift_right_logical(idx, 8)
    rows = lax.broadcasted_iota(jnp.int32, (LO, HP), 0)
    return (rows == lo).astype(jnp.float32).astype(jnp.bfloat16), hi


def forward_kernel(
    x_hbm, w_hbm, lists_hbm, adj_hbm, cot_hbm, coords_hbm,
    own, halo, xs, adj, cot, coords,
    w_ref, lists, proj, packed, fsend, frecv, nsend, nrecv, xsend, xrecv, lsem,
):
    n = lax.axis_index("node")
    f = lax.axis_index("feat")
    y = lax.shift_right_logical(f, 1)
    x_ref = xs.at[y]
    loads = [
        pltpu.make_async_copy(src, dst, lsem.at[i])
        for i, (src, dst) in enumerate(
            [
                (x_hbm, x_ref),
                (w_hbm, w_ref),
                (lists_hbm, lists),
                (coords_hbm, coords),
                (cot_hbm, cot),
                (adj_hbm, adj),
            ]
        )
    ]
    for load in loads:
        load.start()
    barrier = enter(n, f)
    loads[0].wait()
    loads[1].wait()
    wt = w_ref[...].astype(jnp.float32).T.astype(jnp.bfloat16)
    for h in range(GD):
        proj[h] = lax.dot_general(
            wt,
            xs[y, h * LO : (h + 1) * LO, :],
            (((1,), (1,)), ((), ())),
            preferred_element_type=jnp.float32,
        ).astype(jnp.bfloat16)
    pl.semaphore_wait(barrier, NN + NF - 2)

    def feat_copy(k, to, source):
        return pltpu.make_async_remote_copy(
            src_ref=proj.at[:, pl.ds(pl.multiple_of(to * CW, CW), CW), :],
            dst_ref=own.at[pl.ds(source * GD, GD)],
            send_sem=fsend.at[k],
            recv_sem=frecv.at[k],
            device_id={"feat": to},
            device_id_type=MESH,
        )

    def start_feat(k, c):
        feat_copy(k, feat_at(f, k), f).start()
        return c

    lax.fori_loop(1, NF, start_feat, 0)
    loads[2].wait()
    own[pl.ds(f * GD, GD)] = proj[:, pl.ds(pl.multiple_of(f * CW, CW), CW), :]

    def wait_feat(k, c):
        feat_copy(k, feat_at(f, k), feat_back(f, k)).wait_recv()
        return c

    lax.fori_loop(1, NF, wait_feat, 0)

    def rows_copy(k, source):
        return pltpu.make_async_remote_copy(
            src_ref=xs.at[y],
            dst_ref=xs.at[source],
            send_sem=xsend.at[k],
            recv_sem=xrecv.at[k],
            device_id={"feat": feat_at(f, 2 * k)},
            device_id_type=MESH,
        )

    for k in (1, 3):
        rows_copy(k, y).start()

    def pick(lists_at):
        hots = [one_hot_t(lists, p) for p in lists_at]
        hot = jnp.concatenate([h for h, _ in hots], axis=1)
        hi = jnp.concatenate([h for _, h in hots], axis=1)
        got = jnp.zeros((CW, len(hots) * HP), jnp.float32)
        step = 32
        for g in range(0, GP, step):
            part = jnp.dot(
                own[g : g + step].reshape(step * CW, LO), hot, preferred_element_type=jnp.float32
            )
            for h in range(step):
                got = jnp.where(hi == g + h, part[h * CW : (h + 1) * CW], got)
        got = got.astype(jnp.bfloat16)
        return [got[:, i * HP : (i + 1) * HP] for i in range(len(hots))]

    def node_copy(k, to, source):
        return pltpu.make_async_remote_copy(
            src_ref=packed.at[k],
            dst_ref=halo.at[source],
            send_sem=nsend.at[k],
            recv_sem=nrecv.at[k],
            device_id={"node": to},
            device_id_type=MESH,
        )

    def send_some(ks):
        tos = [node_at(n, k) for k in ks]
        for k, to, got in zip(ks, tos, pick(tos)):
            packed[k] = got
            node_copy(k, to, n).start()

    def send_nodes(i, c):
        send_some([far_first(i) * XS + j for j in range(XS)])
        return c

    first = far_first(0) * XS
    send_some([first])
    send_some([first + j for j in range(1, XS)])
    lax.fori_loop(1, ZS - 1, send_nodes, 0)
    tos = [node_at(n, k) for k in range(XS)]
    for k, (to, got) in enumerate(zip(tos, pick(tos))):
        if k == 0:
            halo[n] = got
        else:
            packed[k] = got
            node_copy(k, to, n).start()

    def finish_node(i, c):
        k = NN - i
        node_copy(k, node_at(n, k), node_back(n, k)).wait()
        return c

    lax.fori_loop(1, NN, finish_node, 0)

    def finish_feat(k, c):
        feat_copy(k, feat_at(f, k), f).wait_send()
        return c

    lax.fori_loop(1, NF, finish_feat, 0)
    for k in (1, 3):
        rows_copy(k, (y + NY - k) & (NY - 1)).wait()
    for load in loads[3:]:
        load.wait()


def forward(features, weight, lists, adjacency, cotangent, coords):
    part = jax.ShapeDtypeStruct((GP, CW, LO), jnp.bfloat16)

    def like(a):
        return jax.ShapeDtypeStruct(a.shape, a.dtype)

    return pl.pallas_call(
        forward_kernel,
        out_shape=(
            part,
            part,
            jax.ShapeDtypeStruct((NY, RD, F), jnp.bfloat16),
            like(adjacency),
            like(cotangent),
            like(coords),
        ),
        in_specs=[pl.BlockSpec(memory_space=pltpu.HBM)] * 6,
        out_specs=(pl.BlockSpec(memory_space=VMEM),) * 6,
        scratch_shapes=[
            VMEM((F, F), jnp.bfloat16),
            VMEM((NN, HP), jnp.int32),
            VMEM((GD, F, LO), jnp.bfloat16),
            VMEM((NN, CW, HP), jnp.bfloat16),
            pltpu.SemaphoreType.DMA((NF,)),
            pltpu.SemaphoreType.DMA((NF,)),
            pltpu.SemaphoreType.DMA((NN,)),
            pltpu.SemaphoreType.DMA((NN,)),
            pltpu.SemaphoreType.DMA((NY,)),
            pltpu.SemaphoreType.DMA((NY,)),
            pltpu.SemaphoreType.DMA((6,)),
        ],
        compiler_params=pltpu.CompilerParams(
            collective_id=0, has_side_effects=True, vmem_limit_bytes=12 * 2**20
        ),
        name="project_and_send",
    )(
        *(
            pltpu.with_memory_space_constraint(a, pltpu.HBM)
            for a in (features, weight, lists, adjacency, cotangent, coords)
        )
    )


UNROLL = 256
WIDE = 4


def blocks_kernel(
    coords_v, counts, held, own, halo, cot, act, local, remote, coords, ext, pre, gpre, grad, sem
):
    load = pltpu.make_async_copy(coords_v, coords, sem)
    load.start()
    count = counts[0]
    pre[ROWB] = jnp.zeros((CW, BLK), jnp.float32)
    for g in range(GP):
        for s in range(2):
            ext[2 * g + s] = own[g, :, s * BLK : (s + 1) * BLK]
            ext[ROWB + 2 * g + s] = halo[g, :, s * BLK : (s + 1) * BLK]
    load.wait()

    def row_of(b):
        return jnp.where(b < count, coords[0, b], ROWB)

    def gather(j, c, stored=0):
        base = j * UNROLL
        terms = []
        for b in [base + u for u in range(0, UNROLL, WIDE)]:
            cols = jnp.concatenate([ext[coords[1, b + i]] for i in range(WIDE)], axis=0)
            part = lax.dot_general(
                cols,
                held[pl.ds(b, WIDE)].reshape(WIDE * BLK, BLK),
                NT,
                preferred_element_type=jnp.float32,
            )
            for i in range(WIDE):
                terms.append(part[i * CW : (i + 1) * CW, i * BLK : (i + 1) * BLK])
        for u in range(UNROLL):
            r = row_of(base + u)
            pre[r] = terms[u] if u < stored else pre[r] + terms[u]
        return c

    gather(0, 0, ROWB)
    lax.fori_loop(1, MAXB // UNROLL, gather, 0)

    for r in range(ROWB):
        v = pre[r]
        at = slice(r * BLK, (r + 1) * BLK)
        sigma = jax.nn.sigmoid(v)
        act[:, at] = (v * sigma).astype(jnp.bfloat16)
        gpre[r] = (cot[:, at].astype(jnp.float32) * sigma * (1.0 + v * (1.0 - sigma))).astype(
            jnp.bfloat16
        )
    gpre[ROWB] = jnp.zeros((CW, BLK), jnp.bfloat16)

    def spread(j, c, stored=0):
        base = j * UNROLL
        terms = []
        for b in [base + u for u in range(0, UNROLL, 2)]:
            rows = jnp.concatenate([gpre[row_of(b)], gpre[row_of(b + 1)]], axis=0)
            pair = jnp.dot(
                rows,
                jnp.concatenate([held[b], held[b + 1]], axis=1),
                preferred_element_type=jnp.float32,
            )
            terms += [pair[:CW, :BLK], pair[CW:, BLK:]]
        for u in range(UNROLL):
            col = coords[1, base + u]
            grad[col] = terms[u] if u < stored else grad[col] + terms[u]
        return c

    spread(0, 0, COLB)
    lax.fori_loop(1, MAXB // UNROLL, spread, 0)
    for g in range(GP):
        for s in range(2):
            at = slice(s * BLK, (s + 1) * BLK)
            local[g, :, at] = grad[2 * g + s]
            remote[g, :, at] = grad[ROWB + 2 * g + s].astype(jnp.bfloat16)


def blocks(coords, counts, adjacency, own, halo, cotangent):
    return pl.pallas_call(
        blocks_kernel,
        out_shape=(
            jax.ShapeDtypeStruct((CW, ROWB * BLK), jnp.bfloat16),
            jax.ShapeDtypeStruct((GP, CW, LO), jnp.float32),
            jax.ShapeDtypeStruct((NN, CW, HP), jnp.bfloat16),
        ),
        in_specs=[
            pl.BlockSpec(memory_space=VMEM),
            pl.BlockSpec(memory_space=pltpu.SMEM),
            pl.BlockSpec(memory_space=VMEM),
            pl.BlockSpec(memory_space=VMEM),
            pl.BlockSpec(memory_space=VMEM),
            pl.BlockSpec(memory_space=VMEM),
        ],
        out_specs=(pl.BlockSpec(memory_space=VMEM),) * 3,
        scratch_shapes=[
            pltpu.SMEM((2, MAXB), jnp.int32),
            VMEM((COLB, CW, BLK), jnp.bfloat16),
            VMEM((ROWB + 1, CW, BLK), jnp.float32),
            VMEM((ROWB + 1, CW, BLK), jnp.bfloat16),
            VMEM((COLB, CW, BLK), jnp.float32),
            pltpu.SemaphoreType.DMA,
        ],
        compiler_params=pltpu.CompilerParams(vmem_limit_bytes=14 * 2**20),
        name="blocks",
    )(coords, counts, adjacency, own, halo, cotangent)


def backward_kernel(
    remote, local, lists, xs, w_ref, in_grad, w_grad,
    wt, x_far, x_other, landed, acc, gz, gz_rows, pieces, pland, zpart, zland, whole,
    nsend, nrecv, fsend, frecv, xsend, xrecv, osend, orecv, psend, precv, zsend, zrecv, asend, arecv,
):
    n = lax.axis_index("node")
    f = lax.axis_index("feat")
    y = lax.shift_right_logical(f, 1)
    core = f & 1
    far = y ^ 2
    barrier = enter(n, f)

    def add(lists_at, vals):
        hots = [one_hot_t(lists, p) for p in lists_at]
        hot = jnp.concatenate([h for h, _ in hots], axis=1)
        step = 16
        for g in range(0, GP, step):
            rows = jnp.concatenate(
                [
                    jnp.concatenate(
                        [jnp.where(hi == g + h, v, 0.0).astype(jnp.bfloat16) for h in range(step)],
                        axis=0,
                    )
                    for (_, hi), v in zip(hots, vals)
                ],
                axis=1,
            )
            term = lax.dot_general(rows, hot, NT, preferred_element_type=jnp.float32)
            acc[g : g + step] = acc[g : g + step] + term.reshape(step, CW, LO)

    pl.semaphore_wait(barrier, NN + NF - 2)

    def node_copy(k, to, source):
        return pltpu.make_async_remote_copy(
            src_ref=remote.at[to],
            dst_ref=landed.at[source],
            send_sem=nsend.at[k],
            recv_sem=nrecv.at[k],
            device_id={"node": to},
            device_id_type=MESH,
        )

    for k in range(1, XS):
        node_copy(k, node_at(n, k), n).start()

    def start_nodes(i, c):
        for j in range(XS):
            k = far_first(i) * XS + j
            node_copy(k, node_at(n, k), n).start()
        return c

    lax.fori_loop(0, ZS - 1, start_nodes, 0)
    far_copy = pltpu.make_async_remote_copy(
        src_ref=xs.at[y],
        dst_ref=x_far,
        send_sem=xsend,
        recv_sem=xrecv,
        device_id={"feat": f ^ 4},
        device_id_type=MESH,
    )

    def other_copy(k, src):
        return pltpu.make_async_remote_copy(
            src_ref=src,
            dst_ref=x_other.at[(y + k) & (NY - 1)],
            send_sem=osend.at[k],
            recv_sem=orecv.at[k],
            device_id={"feat": f ^ 1},
            device_id_type=MESH,
        )

    far_copy.start()
    for k in (0, 1, 3):
        other_copy(k, xs.at[(y + k) & (NY - 1)]).start()
    wt[...] = w_ref[...].astype(jnp.float32).T.astype(jnp.bfloat16)
    acc[...] = local[...]
    sources = [node_back(n, k) for k in range(XS)]
    for k in range(1, XS):
        node_copy(k, node_at(n, k), sources[k]).wait_recv()
    landed[n] = remote[n]
    add(sources, [landed[p].astype(jnp.float32) for p in sources])

    def take_nodes(i, c):
        ks = [far_first(i) * XS + j for j in range(XS)]
        sources = [node_back(n, k) for k in ks]
        for k, p in zip(ks, sources):
            node_copy(k, node_at(n, k), p).wait_recv()
        add(sources, [landed[p].astype(jnp.float32) for p in sources])
        return c

    lax.fori_loop(0, ZS - 4, take_nodes, 0)
    far_copy.wait_recv()
    other_copy(2, x_far).start()
    lax.fori_loop(ZS - 4, ZS - 1, take_nodes, 0)
    gz[...] = acc[...].astype(jnp.bfloat16)

    def feat_copy(k, to, source):
        return pltpu.make_async_remote_copy(
            src_ref=gz.at[pl.ds(to * GD, GD)],
            dst_ref=gz_rows.at[:, pl.ds(pl.multiple_of(source * CW, CW), CW), :],
            send_sem=fsend.at[k],
            recv_sem=frecv.at[k],
            device_id={"feat": to},
            device_id_type=MESH,
        )

    def start_feat(k, c):
        feat_copy(k, feat_at(f, k), f).start()
        return c

    lax.fori_loop(1, NF, start_feat, 0)
    for k in range(NY):
        other_copy(k, x_far).wait_recv()

    def product(rows, at, group):
        out = jnp.zeros((CW, F), jnp.float32)
        for j in range(GD):
            out = out + jnp.dot(
                gz[group + j],
                rows[at, j * LO : (j + 1) * LO, :],
                preferred_element_type=jnp.float32,
            )
        return out

    mine = product(x_far.reshape(1, RD, F), 0, GD * (2 * far + core))
    for k in (0, 1, 3):
        at = (y + k) & (NY - 1)
        mine = mine + product(xs, at, GD * (2 * at + core))
    for at in range(NY):
        mine = mine + product(x_other, at, GD * (2 * at + 1 - core))
    mine = mine * (1.0 / math.sqrt(NN * ROWB * BLK))
    z, x = n & -XS, n & (XS - 1)
    pieces[...] = mine.reshape(XS, CW // XS, F)

    def x_at(k):
        return z + ((x + k) & (XS - 1))

    def z_at(k):
        return ((z + XS * k) & (NN - 1)) + x

    def share_copy(k, source):
        to = x_at(k)
        return pltpu.make_async_remote_copy(
            src_ref=pieces.at[to & (XS - 1)],
            dst_ref=pland.at[source & (XS - 1)],
            send_sem=psend.at[k],
            recv_sem=precv.at[k],
            device_id={"node": to},
            device_id_type=MESH,
        )

    for k in range(1, XS):
        share_copy(k, n).start()
    pland[x] = pieces[x]
    for k in range(1, XS):
        share_copy(k, x_at(XS - k)).wait_recv()
    zpart[...] = pland[0] + pland[1] + pland[2] + pland[3]

    def z_copy(k, source):
        return pltpu.make_async_remote_copy(
            src_ref=zpart,
            dst_ref=zland.at[lax.shift_right_logical(source, 2)],
            send_sem=zsend.at[k],
            recv_sem=zrecv.at[k],
            device_id={"node": z_at(k)},
            device_id_type=MESH,
        )

    for k in range(1, ZS):
        z_copy(k, n).start()

    zland[lax.shift_right_logical(n, 2)] = zpart[...]
    for k in range(1, ZS):
        z_copy(k, z_at(ZS - k)).wait_recv()
    summed = zland[0]
    for i in range(1, ZS):
        summed = summed + zland[i]
    whole[x] = summed

    def back_copy(k, source):
        return pltpu.make_async_remote_copy(
            src_ref=whole.at[x],
            dst_ref=whole.at[source & (XS - 1)],
            send_sem=asend.at[k],
            recv_sem=arecv.at[k],
            device_id={"node": x_at(k)},
            device_id_type=MESH,
        )

    for k in range(1, XS):
        back_copy(k, n).start()

    gz_rows[:, pl.ds(pl.multiple_of(f * CW, CW), CW), :] = gz[pl.ds(f * GD, GD)]

    def wait_feat(k, c):
        feat_copy(k, feat_at(f, k), feat_back(f, k)).wait_recv()
        return c

    lax.fori_loop(1, NF, wait_feat, 0)
    for h in range(GD):
        rows = gz_rows[h].astype(jnp.float32).T.astype(jnp.bfloat16)
        in_grad[h * LO : (h + 1) * LO, :] = jnp.dot(
            rows, wt[...], preferred_element_type=jnp.float32
        ).astype(jnp.bfloat16)

    for k in range(1, XS):
        back_copy(k, x_at(XS - k)).wait_recv()
    w_grad[...] = whole[...].reshape(CW, F)
    for k in range(1, XS):
        share_copy(k, n).wait_send()
        back_copy(k, n).wait_send()
    for k in range(1, ZS):
        z_copy(k, n).wait_send()

    def finish_node(k, c):
        node_copy(k, node_at(n, k), n).wait_send()
        return c

    lax.fori_loop(1, NN, finish_node, 0)

    def finish_feat(k, c):
        feat_copy(k, feat_at(f, k), f).wait_send()
        return c

    lax.fori_loop(1, NF, finish_feat, 0)
    far_copy.wait_send()
    for k in range(NY):
        other_copy(k, x_far).wait_send()


def backward(remote, local, lists, xs, weight):
    dma = pltpu.SemaphoreType.DMA
    return pl.pallas_call(
        backward_kernel,
        out_shape=(
            jax.ShapeDtypeStruct((RD, F), jnp.bfloat16),
            jax.ShapeDtypeStruct((CW, F), jnp.float32),
        ),
        in_specs=[
            pl.BlockSpec(memory_space=VMEM),
            pl.BlockSpec(memory_space=VMEM),
            pl.BlockSpec(memory_space=VMEM),
            pl.BlockSpec(memory_space=VMEM),
            pl.BlockSpec(memory_space=VMEM),
        ],
        out_specs=(pl.BlockSpec(memory_space=VMEM),) * 2,
        scratch_shapes=[
            VMEM((F, F), jnp.bfloat16),
            VMEM((RD, F), jnp.bfloat16),
            VMEM((NY, RD, F), jnp.bfloat16),
            VMEM((NN, CW, HP), jnp.bfloat16),
            VMEM((GP, CW, LO), jnp.float32),
            VMEM((GP, CW, LO), jnp.bfloat16),
            VMEM((GD, F, LO), jnp.bfloat16),
            VMEM((XS, CW // XS, F), jnp.float32),
            VMEM((XS, CW // XS, F), jnp.float32),
            VMEM((CW // XS, F), jnp.float32),
            VMEM((ZS, CW // XS, F), jnp.float32),
            VMEM((XS, CW // XS, F), jnp.float32),
            dma((NN,)),
            dma((NN,)),
            dma((NF,)),
            dma((NF,)),
            dma,
            dma,
            dma((NY,)),
            dma((NY,)),
            dma((XS,)),
            dma((XS,)),
            dma((ZS,)),
            dma((ZS,)),
            dma((XS,)),
            dma((XS,)),
        ],
        compiler_params=pltpu.CompilerParams(
            collective_id=1, has_side_effects=True, vmem_limit_bytes=32 * 2**20
        ),
        name="return_and_sum",
    )(remote, local, lists, xs, weight)


def body(features, weight, adjacency, block_coords, block_counts, send_rows, cotangent):
    own, halo, xs, held, cot, coords = forward(
        features, weight, send_rows, adjacency, cotangent, block_coords
    )
    activations, local, remote = blocks(coords, block_counts, held, own, halo, cot)
    input_grad, weight_grad_t = backward(remote, local, send_rows, xs, weight)
    weight_grad = weight_grad_t.T
    return (activations, input_grad, weight_grad)


def solution(mesh):
    return jax.shard_map(
        body,
        mesh=mesh,
        in_specs=(
            P(("node", "feat"), None),
            P(),
            P("node", None, None),
            P(None, "node"),
            P("node"),
            P("node", None),
            P("feat", "node"),
        ),
        out_specs=(P("feat", "node"), P(("node", "feat"), None), P(None, "feat")),
        check_vma=False,
    )
```
